32 devices in a mesh: fsdp: 8 (over y, x, core), tp: 4 (over z).
Axes of the slice: x: 2, y: 2, z: 4, core: 2. Of those that a mesh axis runs over, the one named last changes fastest.
Arguments:
- layer_input: bfloat16 [8192, 2048], P(('fsdp', 'tp')), may hold values from -6 to 6
- norm_gains: float32 [2, 2048], replicated, may hold values from 0.1 to 1.9
- w_qkv: bfloat16 [3, 2048, 2048], P(None, 'fsdp', 'tp'), may hold values from -0.125 to 0.125
- w_out: bfloat16 [2048, 2048], P('tp', 'fsdp'), may hold values from -0.5 to 0.5
- w_gate_up: bfloat16 [2, 2048, 5504], P(None, 'fsdp', 'tp'), may hold values from -0.125 to 0.125
- w_down: bfloat16 [5504, 2048], P('tp', 'fsdp'), may hold values from -0.078125 to 0.078125
- doc_start: int32 [8192], P('fsdp'), may hold values from 0 to 8191, as said below
- out_cotangent: bfloat16 [8192, 2048], P(('fsdp', 'tp')), may hold values from -6 to 6
Outputs:
- layer_output: bfloat16 [8192, 2048], P(('fsdp', 'tp'))
- input_grad: bfloat16 [8192, 2048], P(('fsdp', 'tp'))
- gain_grad: float32 [2, 2048], replicated
- w_qkv_grad: float32 [3, 2048, 2048], P(None, 'fsdp', 'tp')
- w_out_grad: float32 [2048, 2048], P('tp', 'fsdp')
- w_gate_up_grad: float32 [2, 2048, 5504], P(None, 'fsdp', 'tp')
- w_down_grad: float32 [5504, 2048], P('tp', 'fsdp')
The draws below stay inside these ranges and needn't reach their ends.
Inputs may be any that keep to these rules, and one draw needn't show every extreme that they name: Documents are runs of consecutive tokens: doc_start[p] is p or doc_start[p - 1]. A document starts at every multiple of 4096 and at the last position, and never at a position p with p % 1024 < 256 that is not a multiple of 4096.
All inputs are finite; a program needn't handle non-finite values.
Results may differ from the reference program's by a relative error of at most 0.02.
Values may be sent and summed in bfloat16 or wider, within the bound.
No kernel may reach another device: no remote copies, remote signals or barrier semaphores. Data moves between devices by JAX's collectives and lax.ppermute only.
A program may use at most 320 MiB of HBM per device.

```python
import math
import jax
import jax.numpy as jnp
from jax import lax

D = 2048
HEADS = 16
HEAD_DIM = 128
FF = 5504
WINDOW = 1024
SPAN = 1024
SEQ_LEN = 4096
TOKENS = 8192
SEQS = 2
QBLOCK = 512


def draw_doc_start(key, part):
    key = jax.random.fold_in(key, 11)
    rate_key, start_key = jax.random.split(key)
    seq_count = TOKENS // SEQ_LEN
    exponent = jax.random.randint(rate_key, (seq_count,), 3, 13).astype(jnp.int32)
    spacing = jnp.minimum(jnp.left_shift(jnp.ones((seq_count,), jnp.int32), exponent), SEQ_LEN)
    position = jnp.arange(TOKENS, dtype=jnp.int32)
    spacing_tok = spacing[position // SEQ_LEN]
    random_bits = jax.random.randint(start_key, (TOKENS,), 0, 1 << 30).astype(jnp.int32)
    starts = random_bits % spacing_tok == 0
    quiet_zone = position % SPAN < WINDOW // 4
    starts = starts & jnp.logical_not(quiet_zone) | (position % SEQ_LEN == 0) | (position == TOKENS - 1)
    return lax.cummax(jnp.where(starts, position, 0), axis=0).astype(jnp.int32)


def spiked(drawn, rng, source, target, shards_of, factor):
    owner, partner = [(jnp.arange(drawn.shape[axis_at]) // (drawn.shape[axis_at] // shards_of)).reshape([-1 if axis == axis_at else 1 for axis in range(drawn.ndim)]) for axis_at in (source, target)]
    chosen = jax.random.permutation(rng, shards_of)[partner]
    strong = (owner == chosen) | (owner == (partner + shards_of // 2) % shards_of)
    return jnp.where(strong, factor * drawn, drawn)


def block_scale(stream_key, extent, cuts, low, top_value):
    def one(dim, shards_of):
        heights = jax.random.uniform(jax.random.fold_in(jax.random.fold_in(stream_key, 6), dim), (shards_of,), jnp.float32, low / len(cuts), top_value / len(cuts))
        return jnp.repeat(jnp.exp(heights), extent[dim] // shards_of).reshape((-1,) + (1,) * (len(extent) - dim - 1))

    factor_of = one(*cuts[0])
    for cut in cuts[1:]:
        factor_of = factor_of * one(*cut)
    return factor_of


def centred(rng, dims, scale, bound, cuts=(), kind=jnp.bfloat16):
    level = block_scale(rng, dims, cuts, -0.22, 0.18) if cuts else 1.0
    drawn = jax.random.normal(rng, dims, jnp.float32) * scale * level
    return jnp.minimum(jnp.maximum(drawn, -bound), bound).astype(kind)


def heavy_noise(key, shape, scale, limit, cuts, heavy, held_as=jnp.bfloat16):
    array = scale * jax.random.normal(key, shape, jnp.float32)
    if cuts:
        array = array * block_scale(key, shape, cuts, -0.22, 0.18)
    return jnp.clip(spiked(array, jax.random.fold_in(key, 3), *heavy), -limit, limit).astype(held_as)


def setup_inputs(seed: int = 0) -> dict:
    key_list = jax.random.split(jax.random.key(seed), 9)
    layer_input = centred(key_list[0], (TOKENS, D), 1.0, 6.0, ((0, 32),))
    norm_gains = jnp.clip(1.0 + 0.18 * jax.random.normal(key_list[1], (2, D), jnp.float32), 0.1, 1.9)
    w_qkv = centred(key_list[2], (3, D, D), D ** -0.5, 0.125, ((1, 8), (2, 4)))
    w_out = centred(key_list[3], (D, D), (D // 16) ** -0.5, 0.5, ((0, 4), (1, 8)))
    w_gate_up = centred(key_list[4], (2, D, FF), D ** -0.5, 0.125, ((1, 8), (2, 4)))
    w_down = centred(key_list[5], (FF, D), FF ** -0.5, 0.078125, ((0, 4), (1, 8)))
    doc_start = draw_doc_start(jax.random.fold_in(key_list[8], 71), 0)
    out_cotangent = heavy_noise(key_list[7], (TOKENS, D), 1.0, 6.0, ((0, 32),), (0, 1, 32, 2.75))
    return {"layer_input": layer_input, "norm_gains": norm_gains, "w_qkv": w_qkv, "w_out": w_out, "w_gate_up": w_gate_up, "w_down": w_down, "doc_start": doc_start, "out_cotangent": out_cotangent}


EPS = 1e-06
MASKED = -1e+30
HIGHEST = lax.Precision.HIGHEST

@jax.custom_vjp
def low(v):
    return lax.optimization_barrier(v.astype(jnp.bfloat16)).astype(jnp.float32)

@jax.custom_vjp
def low_back(v):
    return v

def low_keep(v):
    return (low(v), None)

def low_pass(kept, grad):
    return (grad,)

def back_keep(v):
    return (v, None)

def back_low(kept, grad):
    return (low(grad),)
low.defvjp(low_keep, low_pass)
low_back.defvjp(back_keep, back_low)

def normed(values, gain):
    return values * lax.rsqrt(lax.optimization_barrier(jnp.mean(values * values, axis=-1, keepdims=True)) + EPS) * gain

def attention(queries, key_rows, value_rows, doc_local):
    padding = jnp.zeros((WINDOW, HEADS, HEAD_DIM), jnp.float32)
    keys_padded = jnp.concatenate([padding, key_rows], axis=0)
    values_padded = jnp.concatenate([padding, value_rows], axis=0)
    scale = 1.0 / math.sqrt(HEAD_DIM)

    def one_block(first_row):
        q_block = lax.dynamic_slice_in_dim(queries, first_row, QBLOCK, 0)
        k_block = lax.dynamic_slice_in_dim(keys_padded, first_row, WINDOW + QBLOCK, 0)
        v_block = lax.dynamic_slice_in_dim(values_padded, first_row, WINDOW + QBLOCK, 0)
        doc_block = lax.dynamic_slice_in_dim(doc_local, first_row, QBLOCK, 0)
        query_pos = first_row + jnp.arange(QBLOCK, dtype=jnp.int32)
        key_pos = first_row - WINDOW + jnp.arange(WINDOW + QBLOCK, dtype=jnp.int32)
        allowed = (key_pos[None, :] <= query_pos[:, None]) & (key_pos[None, :] > query_pos[:, None] - WINDOW) & (key_pos[None, :] >= doc_block[:, None])
        scores = low_back(jnp.einsum('qhe,khe->hqk', q_block, k_block, precision=HIGHEST) * scale)
        scores = jnp.where(allowed[None], scores, MASKED)
        row_max = lax.optimization_barrier(jnp.max(scores, axis=-1, keepdims=True))
        exponent = jnp.exp(scores - row_max)
        probs = exponent / lax.optimization_barrier(jnp.sum(exponent, axis=-1, keepdims=True))
        return jnp.einsum('hqk,khe->qhe', low(probs), v_block, precision=HIGHEST)
    starts = (jnp.arange(SEQ_LEN // QBLOCK) * QBLOCK).astype(jnp.int32)
    pieces = lax.map(jax.checkpoint(one_block), starts)
    return pieces.reshape(SEQ_LEN, HEADS * HEAD_DIM)

def layer_forward(layer_in, gains, w_qkv, w_out, w_gate_up, w_down, doc_local):
    normed_one = low(normed(layer_in, gains[0]))
    qkv = low(low_back(jnp.einsum('td,sde->ste', normed_one, w_qkv, precision=HIGHEST)))
    head_shape = (SEQ_LEN, HEADS, HEAD_DIM)
    mixed = attention(qkv[0].reshape(head_shape), qkv[1].reshape(head_shape), qkv[2].reshape(head_shape), doc_local)
    heads_out = low(low_back(mixed))
    attention_out = low_back(jnp.dot(heads_out, w_out, precision=HIGHEST))
    residual_mid = layer_in + attention_out
    normed_two = low(normed(residual_mid, gains[1]))
    gate_up = low_back(jnp.einsum('td,sdf->stf', normed_two, w_gate_up, precision=HIGHEST))
    gate_pre = gate_up[0]
    act = low(gate_pre * jax.nn.sigmoid(gate_pre) * gate_up[1])
    return residual_mid + low_back(jnp.dot(act, w_down, precision=HIGHEST))

def reference(layer_input, norm_gains, w_qkv, w_out, w_gate_up, w_down, doc_start, out_cotangent):
    params = (layer_input.astype(jnp.float32), norm_gains.astype(jnp.float32), w_qkv.astype(jnp.float32), w_out.astype(jnp.float32), w_gate_up.astype(jnp.float32), w_down.astype(jnp.float32))
    seq_bases = (jnp.arange(SEQS) * SEQ_LEN).astype(jnp.int32)
    doc_seqs = doc_start.astype(jnp.int32).reshape(SEQS, SEQ_LEN)

    def whole_batch(layer_in, gains, wq, wo, wgu, wd):

        def one_sequence(sequence_item):
            rows_in, docs, seq_base = sequence_item
            return layer_forward(rows_in, gains, wq, wo, wgu, wd, docs - seq_base)
        outs = lax.map(jax.checkpoint(one_sequence), (layer_in.reshape(SEQS, SEQ_LEN, D), doc_seqs, seq_bases))
        return outs.reshape(TOKENS, D)
    result, pullback = jax.vjp(whole_batch, *params)
    gradients = pullback(out_cotangent.astype(jnp.float32))
    return (result.astype(jnp.bfloat16), gradients[0].astype(jnp.bfloat16), gradients[1], gradients[2], gradients[3], gradients[4], gradients[5])
```

```python
import functools
import math

import jax
import jax.numpy as jnp
from jax import lax
from jax.experimental import pallas as pl
from jax.experimental.pallas import tpu as pltpu
from jax.sharding import PartitionSpec as P

HEAD_DIM = 128
WINDOW = 1024
SEQ_LEN = 4096
QB = 256
SCALE = 1.0 / math.sqrt(HEAD_DIM)
LOG2E = 1.4426950408889634
EPS = 1e-06
MASKED = -1e30
NT = (((1,), (1,)), ((), ()))

def nt(a, b): return lax.dot_general(a, b, NT, preferred_element_type=jnp.float32)
def nn(a, b): return jnp.dot(a, b, preferred_element_type=jnp.float32)

def masked_scores(k_j, q, j, lo):
    s = nt(k_j, q)
    row = lax.broadcasted_iota(jnp.int32, s.shape, 0) + j * QB
    ok = row >= lo
    if (j + 1) * QB > WINDOW:
        hi = lax.broadcasted_iota(jnp.int32, (1, QB), 1) + WINDOW
        ok = ok & (row <= hi)
    return jnp.where(ok, s, MASKED)

def low_bound(doc_ref, b, off):
    q_row = lax.broadcasted_iota(jnp.int32, (1, QB), 1)
    doc = doc_ref[:, b * QB:(b + 1) * QB]
    return jnp.maximum(q_row + 1, doc - off + (WINDOW - b * QB))

def attend_kernel(off_ref, doc_ref, q_ref, kp_ref, vp_ref, ko_ref, vo_ref, o_ref, lse_ref, k_s, vt_s):
    h = pl.program_id(0)
    off = off_ref[0]
    span = q_ref.shape[0]
    k_s[:WINDOW] = kp_ref[...]
    k_s[WINDOW:] = ko_ref[...]
    vt_s[:, :WINDOW] = vp_ref[...].T
    vt_s[:, WINDOW:] = vo_ref[...].T
    c = SCALE * LOG2E
    n = WINDOW // QB + 1
    for b in range(span // QB):
        q = q_ref[b * QB:(b + 1) * QB]
        lo = low_bound(doc_ref, b, off)
        ss = [masked_scores(k_s[(b + j) * QB:(b + j + 1) * QB], q, j, lo) for j in range(n)]
        m = functools.reduce(jnp.maximum, [jnp.max(s, axis=0, keepdims=True) for s in ss])
        l = jnp.zeros((1, QB), jnp.float32)
        acc = jnp.zeros((HEAD_DIM, QB), jnp.float32)
        for j in range(n):
            p = jnp.exp2((ss[j] - m) * c)
            l = l + jnp.sum(p, axis=0, keepdims=True)
            acc = acc + nn(vt_s[:, (b + j) * QB:(b + j + 1) * QB], p.astype(jnp.bfloat16))
        o_ref[b * QB:(b + 1) * QB] = (acc / l).T.astype(o_ref.dtype)
        lse_ref[pl.ds(h, 1), b * QB:(b + 1) * QB] = m * c + jnp.log2(l)

def back_kernel(off_ref, doc_ref, lse_ref, q_ref, do_ref, kp_ref, vp_ref, ko_ref, vo_ref,
                dq_ref, dkp_ref, dvp_ref, dko_ref, dvo_ref, k_s, v_s, kt_s, dk_s, dv_s):
    h = pl.program_id(0)
    off = off_ref[0]
    span = q_ref.shape[0]
    k_s[:WINDOW] = kp_ref[...]
    k_s[WINDOW:] = ko_ref[...]
    v_s[:WINDOW] = vp_ref[...]
    v_s[WINDOW:] = vo_ref[...]
    kt_s[:, :WINDOW] = kp_ref[...].T
    kt_s[:, WINDOW:] = ko_ref[...].T
    c = SCALE * LOG2E
    n = WINDOW // QB + 1
    seen = 0
    for b in range(span // QB):
        q = q_ref[b * QB:(b + 1) * QB]
        do = do_ref[b * QB:(b + 1) * QB]
        lse = lse_ref[pl.ds(h, 1), b * QB:(b + 1) * QB]
        lo = low_bound(doc_ref, b, off)
        delta = jnp.zeros((1, QB), jnp.float32)
        ps, dps = [], []
        for j in range(n):
            rows = slice((b + j) * QB, (b + j + 1) * QB)
            s = masked_scores(k_s[rows], q, j, lo)
            p = jnp.exp2(s * c - lse)
            dp = nt(v_s[rows], do)
            delta = delta + jnp.sum(p * dp, axis=0, keepdims=True)
            dv = nn(p.astype(jnp.bfloat16), do)
            if b + j >= seen:
                dv_s[rows] = dv
            else:
                dv_s[rows] += dv
            ps.append(p); dps.append(dp)
        dqt = jnp.zeros((HEAD_DIM, QB), jnp.float32)
        for j in range(n):
            rows = slice((b + j) * QB, (b + j + 1) * QB)
            ds = (ps[j] * (dps[j] - delta)).astype(jnp.bfloat16)
            dk = nn(ds, q)
            if b + j >= seen:
                dk_s[rows] = dk
            else:
                dk_s[rows] += dk
            dqt = dqt + nn(kt_s[:, rows], ds)
        seen = b + n
        dq_ref[b * QB:(b + 1) * QB] = (dqt * SCALE).T.astype(dq_ref.dtype)
    dkp_ref[...] = (dk_s[:WINDOW] * SCALE).astype(dkp_ref.dtype)
    dvp_ref[...] = dv_s[:WINDOW].astype(dvp_ref.dtype)
    dko_ref[...] = dk_s[WINDOW:] * SCALE
    dvo_ref[...] = dv_s[WINDOW:]

def head_spec(rows): return pl.BlockSpec((rows, HEAD_DIM), lambda h: (0, h))
def whole(shape): return pl.BlockSpec(shape, lambda h: (0, 0))

def attend(off, doc, q, kp, vp, ko, vo):
    span, width = q.shape
    heads = width // HEAD_DIM
    return pl.pallas_call(
        attend_kernel, grid=(heads,),
        in_specs=[pl.BlockSpec(memory_space=pltpu.SMEM), whole((1, span)), head_spec(span), head_spec(WINDOW), head_spec(WINDOW), head_spec(span), head_spec(span)],
        out_specs=[head_spec(span), whole((heads, span))],
        out_shape=[jax.ShapeDtypeStruct((span, width), jnp.bfloat16), jax.ShapeDtypeStruct((heads, span), jnp.float32)],
        scratch_shapes=[pltpu.VMEM((WINDOW + span, HEAD_DIM), jnp.bfloat16), pltpu.VMEM((HEAD_DIM, WINDOW + span), jnp.bfloat16)],
        compiler_params=pltpu.CompilerParams(vmem_limit_bytes=40 << 20),
        cost_estimate=pl.CostEstimate(flops=4 * heads * span * 1280 * HEAD_DIM, bytes_accessed=6 * span * width * 2, transcendentals=heads * span * 1280),
    )(off, doc, q, kp, vp, ko, vo)

def attend_back(off, doc, lse, q, do, kp, vp, ko, vo):
    span, width = q.shape
    heads = width // HEAD_DIM
    bf, f32 = jnp.bfloat16, jnp.float32
    sd = lambda rows, t: jax.ShapeDtypeStruct((rows, width), t)
    return pl.pallas_call(
        back_kernel, grid=(heads,),
        in_specs=[pl.BlockSpec(memory_space=pltpu.SMEM), whole((1, span)), whole((heads, span)), head_spec(span), head_spec(span), head_spec(WINDOW), head_spec(WINDOW), head_spec(span), head_spec(span)],
        out_specs=[head_spec(span), head_spec(WINDOW), head_spec(WINDOW), head_spec(span), head_spec(span)],
        out_shape=[sd(span, bf), sd(WINDOW, bf), sd(WINDOW, bf), sd(span, f32), sd(span, f32)],
        scratch_shapes=[pltpu.VMEM((WINDOW + span, HEAD_DIM), bf)] * 2 + [pltpu.VMEM((HEAD_DIM, WINDOW + span), bf)] + [pltpu.VMEM((WINDOW + span, HEAD_DIM), f32)] * 2,
        compiler_params=pltpu.CompilerParams(vmem_limit_bytes=40 << 20),
        cost_estimate=pl.CostEstimate(flops=10 * heads * span * 1280 * HEAD_DIM, bytes_accessed=14 * span * width * 2, transcendentals=heads * span * 1280),
    )(off, doc, lse, q, do, kp, vp, ko, vo)

PAIRS = [(0, 1), (1, 0), (2, 3), (3, 2)]
MIDDLE = [(1, 2), (2, 1)]
OUTWARD = [(1, 0), (2, 3)]
INWARD = [(0, 1), (3, 2)]


def is_middle():
    me = lax.axis_index("tp")
    return (me == 1) | (me == 2)


def send(block, route, axis="tp"):
    return lax.ppermute(block, axis, route)


def gather_rows(block):
    me = lax.axis_index("tp")
    rows = block.shape[0]
    mid = is_middle()
    one = send(block, PAIRS)
    near = send(block, MIDDLE)
    far = send(one, MIDDLE)
    two = jnp.where(mid, far, send(near, OUTWARD))
    three = jnp.where(mid, near, send(far, OUTWARD))
    whole_rows = jnp.zeros((4 * rows,) + block.shape[1:], block.dtype)
    for k, part in enumerate((block, one, two, three)):
        whole_rows = lax.dynamic_update_slice_in_dim(whole_rows, part, (me ^ k) * rows, 0)
    return whole_rows


def scatter_rows(part_of):
    three = part_of(3)
    t1 = send(three, INWARD)
    two = part_of(2)
    t2 = send(two, INWARD)
    t3 = send(two + t1, MIDDLE)
    one = part_of(1)
    t4 = send(three + t2, MIDDLE)
    t5 = send(one + t3, PAIRS)
    own = part_of(0)
    f32 = jnp.float32
    return own.astype(f32) + t4.astype(f32) + t5.astype(f32)


def row_parts(partial):
    me = lax.axis_index("tp")
    rows = partial.shape[0] // 4
    return lambda k: lax.dynamic_slice_in_dim(partial, (me ^ k) * rows, rows, 0)


def sum_everywhere(values):
    for axis in ("tp", "fsdp"):
        size = lax.axis_size(axis)
        step = 1
        while step < size:
            values = values + send(values, [(i, i ^ step) for i in range(size)], axis)
            step *= 2
    return values


def behind_route(axis, distance, per_seq):
    size = lax.axis_size(axis)
    pairs = [(i - 1, i) for i in range(1, size) if i % per_seq]
    return pairs if distance > 0 else [(b, a) for a, b in pairs]


def normalize(values):
    inverse = lax.rsqrt(jnp.mean(values * values, axis=-1, keepdims=True) + EPS)
    return (values * inverse, inverse)


def norm_back(grad, gain, unit, inverse):
    scaled = grad * gain
    return inverse * (scaled - unit * jnp.mean(scaled * unit, axis=-1, keepdims=True))


def per_device(layer_input, norm_gains, w_qkv, w_out, w_gate_up, w_down, doc_start, out_cotangent):
    bf, f32 = jnp.bfloat16, jnp.float32
    span_len = doc_start.shape[0]
    offset = (lax.axis_index("fsdp") * span_len).astype(jnp.int32).reshape(1)
    doc_row = doc_start.reshape(1, span_len)
    per_seq = SEQ_LEN // span_len
    full_qkv = lax.all_gather(w_qkv, "fsdp", axis=1, tiled=True)
    full_out = lax.all_gather(w_out, "fsdp", axis=1, tiled=True)
    full_gate_up = lax.all_gather(w_gate_up, "fsdp", axis=1, tiled=True)
    full_down = lax.all_gather(w_down, "fsdp", axis=1, tiled=True)
    input_f32 = layer_input.astype(f32)
    unit_one, inverse_one = normalize(input_f32)
    normed_one = (unit_one * norm_gains[0]).astype(bf)
    attn_rows = gather_rows(normed_one)
    cot_rows = gather_rows(out_cotangent)
    keys = nn(attn_rows, full_qkv[1]).astype(bf)
    values = nn(attn_rows, full_qkv[2]).astype(bf)
    prev_k = send(keys, behind_route("fsdp", 1, per_seq), "fsdp")
    prev_v = send(values, behind_route("fsdp", 1, per_seq), "fsdp")
    queries = nn(attn_rows, full_qkv[0]).astype(bf)
    heads_out, lse = attend(offset, doc_row, queries, prev_k, prev_v, keys, values)
    attn_part = nn(heads_out, full_out).astype(bf)
    residual_mid = input_f32 + scatter_rows(row_parts(attn_part))
    unit_two, inverse_two = normalize(residual_mid)
    normed_two = (unit_two * norm_gains[1]).astype(bf)
    mlp_rows = gather_rows(normed_two)
    gate_up = jnp.einsum("td,sdf->stf", mlp_rows, full_gate_up, preferred_element_type=f32)
    gate_pre = gate_up[0]
    up_pre = gate_up[1]
    sigmoid_gate = jax.nn.sigmoid(gate_pre)
    act = (gate_pre * sigmoid_gate * up_pre).astype(bf)
    contract_first = (((0,), (0,)), ((), ()))
    contract_last = (((1,), (1,)), ((), ()))
    grad_act = lax.dot_general(cot_rows, full_down, contract_last, preferred_element_type=f32)
    grad_up = grad_act * gate_pre * sigmoid_gate
    grad_gate = grad_act * up_pre * sigmoid_gate * (1.0 + gate_pre * (1.0 - sigmoid_gate))
    grad_gate_up = jnp.stack([grad_gate, grad_up]).astype(bf)
    gn2_part = jnp.einsum("stf,sdf->td", grad_gate_up, full_gate_up, preferred_element_type=f32)
    grad_normed_two = scatter_rows(row_parts(gn2_part.astype(bf)))
    down_part = nn(act, full_down).astype(bf)
    layer_output = (residual_mid + scatter_rows(row_parts(down_part))).astype(bf)
    down_grad = lax.dot_general(act, cot_rows, contract_first, preferred_element_type=f32)
    gate_up_grad = jnp.einsum("td,stf->sdf", mlp_rows, grad_gate_up, preferred_element_type=f32)
    grad_mid = out_cotangent.astype(f32) + norm_back(
        grad_normed_two, norm_gains[1], unit_two, inverse_two
    )
    grad_branch = gather_rows(grad_mid.astype(bf))
    grad_heads = lax.dot_general(
        grad_branch, full_out, contract_last, preferred_element_type=f32
    ).astype(bf)
    out_grad = lax.dot_general(heads_out, grad_branch, contract_first, preferred_element_type=f32)
    grad_q, prev_dk, prev_dv, own_dk, own_dv = attend_back(
        offset, doc_row, lse, queries, grad_heads, prev_k, prev_v, keys, values
    )
    back_route = behind_route("fsdp", -1, per_seq)
    grad_k = (own_dk + send(prev_dk, back_route, "fsdp").astype(f32)).astype(bf)
    grad_v = (own_dv + send(prev_dv, back_route, "fsdp").astype(f32)).astype(bf)
    grad_qkv = jnp.stack([grad_q, grad_k, grad_v])
    gn1_part = jnp.einsum("ste,sde->td", grad_qkv, full_qkv, preferred_element_type=f32)
    gn1_part = gn1_part.astype(bf)
    grad_normed_one = scatter_rows(row_parts(gn1_part))
    qkv_grad = jnp.einsum("td,ste->sde", attn_rows, grad_qkv, preferred_element_type=f32)
    input_grad = (
        grad_mid + norm_back(grad_normed_one, norm_gains[0], unit_one, inverse_one)
    ).astype(bf)
    gain_one = jnp.sum(gn1_part.astype(f32) * attn_rows.astype(f32), axis=0) / norm_gains[0]
    gain_two = jnp.sum(grad_normed_two * unit_two, axis=0)
    gain_grad = sum_everywhere(jnp.stack([gain_one, gain_two]))
    owned = [
        lax.psum_scatter(g.astype(bf), "fsdp", scatter_dimension=1, tiled=True).astype(f32)
        for g in (down_grad, gate_up_grad, out_grad, qkv_grad)
    ]
    return (layer_output, input_grad, gain_grad, owned[3], owned[2], owned[1], owned[0])


def solution(mesh):
    in_specs = (
        P(("fsdp", "tp"), None),
        P(),
        P(None, "fsdp", "tp"),
        P("tp", "fsdp"),
        P(None, "fsdp", "tp"),
        P("tp", "fsdp"),
        P("fsdp"),
        P(("fsdp", "tp"), None),
    )
    out_specs = (
        P(("fsdp", "tp"), None),
        P(("fsdp", "tp"), None),
        P(),
        P(None, "fsdp", "tp"),
        P("tp", "fsdp"),
        P(None, "fsdp", "tp"),
        P("tp", "fsdp"),
    )
    return jax.shard_map(
        per_device, mesh=mesh, in_specs=in_specs, out_specs=out_specs, check_vma=False
    )
```

```python
import functools
import math

import jax
import jax.numpy as jnp
from jax import lax
from jax.experimental import pallas as pl
from jax.experimental.pallas import tpu as pltpu
from jax.sharding import PartitionSpec as P

HEAD_DIM = 128
WINDOW = 1024
SEQ_LEN = 4096
QB = 256
SCALE = 1.0 / math.sqrt(HEAD_DIM)
LOG2E = 1.4426950408889634
EPS = 1e-06
MASKED = -1e30
VMEM_LIMIT = 60 << 20
SMALL = pl.CostEstimate(flops=1 << 20, bytes_accessed=1 << 16, transcendentals=0)
NT = (((1,), (1,)), ((), ()))
TN = (((0,), (0,)), ((), ()))


def nt(a, b):
    return lax.dot_general(a, b, NT, preferred_element_type=jnp.float32)


def nn(a, b):
    return jnp.dot(a, b, preferred_element_type=jnp.float32)


def tn(a, b):
    return lax.dot_general(a, b, TN, preferred_element_type=jnp.float32)


def masked_scores(k_j, q, j, lo):
    s = nt(k_j, q)
    row = lax.broadcasted_iota(jnp.int32, s.shape, 0) + j * QB
    ok = row >= lo
    if (j + 1) * QB > WINDOW:
        hi = lax.broadcasted_iota(jnp.int32, (1, QB), 1) + WINDOW
        ok = ok & (row <= hi)
    return jnp.where(ok, s, MASKED)


def low_bound(doc_ref, b, off):
    q_row = lax.broadcasted_iota(jnp.int32, (1, QB), 1)
    doc = doc_ref[:, b * QB : (b + 1) * QB]
    return jnp.maximum(q_row + 1, doc - off + (WINDOW - b * QB))


def block_at(index):
    return pl.ds(pl.multiple_of(index * QB, QB), QB)


def attend_kernel(place_ref, doc_ref, *refs):
    new, old = refs[:4], refs[4:8]
    o_ref, lse_ref, q_s, k_s, vt_s = refs[8:]
    h = pl.program_id(0)
    off, me = place_ref[0], place_ref[1]
    blocks = len(new)
    for slot in range(blocks):
        at = me ^ slot
        q_s[block_at(at)] = new[slot][0]
        k_s[block_at(at)] = old[slot][0]
        k_s[block_at(at + blocks)] = new[slot][1]
        vt_s[:, block_at(at)] = old[slot][1].T
        vt_s[:, block_at(at + blocks)] = new[slot][2].T
    c = SCALE * LOG2E
    n = WINDOW // QB + 1
    for b in range(blocks):
        q = q_s[b * QB : (b + 1) * QB]
        lo = low_bound(doc_ref, b, off)
        ss = [
            masked_scores(k_s[(b + j) * QB : (b + j + 1) * QB], q, j, lo) for j in range(n)
        ]
        m = functools.reduce(jnp.maximum, [jnp.max(s, axis=0, keepdims=True) for s in ss])
        total = jnp.zeros((1, QB), jnp.float32)
        acc = jnp.zeros((HEAD_DIM, QB), jnp.float32)
        for j in range(n):
            p = jnp.exp2((ss[j] - m) * c)
            total = total + jnp.sum(p, axis=0, keepdims=True)
            acc = acc + nn(vt_s[:, (b + j) * QB : (b + j + 1) * QB], p.astype(jnp.bfloat16))
        o_ref[block_at(me ^ b)] = (acc / total).T.astype(o_ref.dtype)
        lse_ref[pl.ds(h, 1), b * QB : (b + 1) * QB] = m * c + jnp.log2(total)


def back_kernel(first, place_ref, doc_ref, lse_ref, *refs):
    new, old, cot = refs[:4], refs[4:8], refs[8:12]
    dq_ref, dk_ref, dv_ref, prev_ref, q_s, do_s, k_s, v_s, kt_s, dk_s, dv_s = refs[-11:]
    h = pl.program_id(0)
    off, me = place_ref[0], place_ref[1]
    blocks = len(new)
    for slot in range(blocks):
        at = me ^ slot
        q_s[block_at(at)] = new[slot][0]
        do_s[block_at(at)] = cot[slot][...]
        k_s[block_at(at)] = old[slot][0]
        k_s[block_at(at + blocks)] = new[slot][1]
        v_s[block_at(at)] = old[slot][1]
        v_s[block_at(at + blocks)] = new[slot][2]
        kt_s[:, block_at(at)] = old[slot][0].T
        kt_s[:, block_at(at + blocks)] = new[slot][1].T
    c = SCALE * LOG2E
    n = WINDOW // QB + 1
    seen = 0
    for b in range(blocks):
        q = q_s[b * QB : (b + 1) * QB]
        do = do_s[b * QB : (b + 1) * QB]
        lse = lse_ref[pl.ds(h + first, 1), b * QB : (b + 1) * QB]
        lo = low_bound(doc_ref, b, off)
        delta = jnp.zeros((1, QB), jnp.float32)
        ps, dps = [], []
        for j in range(n):
            rows = slice((b + j) * QB, (b + j + 1) * QB)
            p = jnp.exp2(masked_scores(k_s[rows], q, j, lo) * c - lse)
            dp = nt(v_s[rows], do)
            delta = delta + jnp.sum(p * dp, axis=0, keepdims=True)
            dv = nn(p.astype(jnp.bfloat16), do)
            if b + j >= seen:
                dv_s[rows] = dv
            else:
                dv_s[rows] += dv
            ps.append(p)
            dps.append(dp)
        dqt = jnp.zeros((HEAD_DIM, QB), jnp.float32)
        for j in range(n):
            rows = slice((b + j) * QB, (b + j + 1) * QB)
            ds = (ps[j] * (dps[j] - delta)).astype(jnp.bfloat16)
            dk = nn(ds, q)
            if b + j >= seen:
                dk_s[rows] = dk
            else:
                dk_s[rows] += dk
            dqt = dqt + nn(kt_s[:, rows], ds)
        seen = b + n
        dq_ref[block_at(me ^ b)] = (dqt * SCALE).T.astype(dq_ref.dtype)
    for slot in range(blocks):
        at = me ^ slot
        rows = slice(slot * QB, (slot + 1) * QB)
        prev_ref[0, rows] = (dk_s[block_at(at)] * SCALE).astype(prev_ref.dtype)
        prev_ref[1, rows] = dv_s[block_at(at)].astype(prev_ref.dtype)
        dk_ref[rows] = dk_s[block_at(at + blocks)] * SCALE
        dv_ref[rows] = dv_s[block_at(at + blocks)]


def spec2(rows, first=0):
    return pl.BlockSpec((rows, HEAD_DIM), lambda h: (0, h + first))


def spec3(count, rows, first=0):
    return pl.BlockSpec((count, rows, HEAD_DIM), lambda h: (0, 0, h + first))


def constant(shape):
    return pl.BlockSpec(shape, lambda h: (0, 0))


def attend(place, doc, new, old):
    blocks = len(new)
    span, width = blocks * QB, new[0].shape[-1]
    heads = width // HEAD_DIM
    bf = jnp.bfloat16
    return pl.pallas_call(
        attend_kernel,
        grid=(heads,),
        in_specs=[pl.BlockSpec(memory_space=pltpu.SMEM), constant((1, span))]
        + [spec3(3, QB)] * blocks
        + [spec3(2, QB)] * blocks,
        out_specs=[spec2(span), constant((heads, span))],
        out_shape=[
            jax.ShapeDtypeStruct((span, width), bf),
            jax.ShapeDtypeStruct((heads, span), jnp.float32),
        ],
        scratch_shapes=[
            pltpu.VMEM((span, HEAD_DIM), bf),
            pltpu.VMEM((WINDOW + span, HEAD_DIM), bf),
            pltpu.VMEM((HEAD_DIM, WINDOW + span), bf),
        ],
        compiler_params=pltpu.CompilerParams(vmem_limit_bytes=VMEM_LIMIT),
        cost_estimate=SMALL,
    )(place, doc, *new, *old)


def attend_back(place, doc, lse, new, old, cot, first, heads, kept=()):
    blocks = len(new)
    span, width = blocks * QB, new[0].shape[-1]
    bf, f32 = jnp.bfloat16, jnp.float32
    fixed = 3 + 3 * blocks
    return pl.pallas_call(
        functools.partial(back_kernel, first),
        grid=(heads,),
        in_specs=[
            pl.BlockSpec(memory_space=pltpu.SMEM),
            constant((1, span)),
            constant(lse.shape),
        ]
        + [spec3(3, QB, first)] * blocks
        + [spec3(2, QB, first)] * blocks
        + [spec2(QB, first)] * blocks
        + [pl.BlockSpec(memory_space=pl.ANY)] * len(kept),
        out_specs=[spec2(span, first)] * 3 + [spec3(2, WINDOW)],
        out_shape=[
            jax.ShapeDtypeStruct((span, width), bf),
            jax.ShapeDtypeStruct((span, width), f32),
            jax.ShapeDtypeStruct((span, width), f32),
            jax.ShapeDtypeStruct((2, WINDOW, heads * HEAD_DIM), bf),
        ],
        input_output_aliases={fixed + i: i for i in range(len(kept))},
        scratch_shapes=[pltpu.VMEM((span, HEAD_DIM), bf)] * 2
        + [pltpu.VMEM((WINDOW + span, HEAD_DIM), bf)] * 2
        + [pltpu.VMEM((HEAD_DIM, WINDOW + span), bf)]
        + [pltpu.VMEM((WINDOW + span, HEAD_DIM), f32)] * 2,
        compiler_params=pltpu.CompilerParams(vmem_limit_bytes=VMEM_LIMIT),
        cost_estimate=SMALL,
    )(place, doc, lse, *new, *old, *cot, *kept)


PAIRS = [(0, 1), (1, 0), (2, 3), (3, 2)]
MIDDLE = [(1, 2), (2, 1)]
OUTWARD = [(1, 0), (2, 3)]
INWARD = [(0, 1), (3, 2)]


def send(block, route, axis="tp"):
    return lax.ppermute(block, axis, route)


def tie(*values):
    return lax.optimization_barrier(values)


def after(value, *others):
    return lax.optimization_barrier((value,) + others)[0]


def flip(bit, axis="fsdp"):
    return [(i, i ^ bit) for i in range(lax.axis_size(axis))]


def neighbour_route(distance, per_seq):
    size = lax.axis_size("fsdp")
    pairs = [(i - 1, i) for i in range(1, size) if i % per_seq]
    return pairs if distance > 0 else [(b, a) for a, b in pairs]


def pick(array, index, axis):
    return lax.dynamic_index_in_dim(array, index, axis, keepdims=False)


def normalize(values):
    inverse = lax.rsqrt(jnp.mean(values * values, axis=-1, keepdims=True) + EPS)
    return (values * inverse, inverse)


def norm_back(grad, gain, unit, inverse):
    scaled = grad * gain
    return inverse * (scaled - unit * jnp.mean(scaled * unit, axis=-1, keepdims=True))


def add(a, b):
    return (a.astype(jnp.float32) + b.astype(jnp.float32)).astype(jnp.bfloat16)


def grad_kernel(blocks, which_ref, *refs):
    lhs, rhs = refs[:blocks], refs[blocks : 2 * blocks]
    away_ref, kept_ref, lhs_s, rhs_s = refs[2 * blocks :]
    count, e = away_ref.shape[1:3]
    group, groups = pl.program_id(0), pl.num_programs(0) // 2

    @pl.when(group == 0)
    def _():
        for k in range(blocks):
            for s in range(count):
                rhs_s[s * e : (s + 1) * e, k * QB : (k + 1) * QB] = rhs[k][s].T

    for k in range(blocks):
        lhs_s[k * QB : (k + 1) * QB] = lhs[k][...]

    def product(out_ref):
        for s in range(count):
            out_ref[0, s] = nn(rhs_s[s * e : (s + 1) * e], lhs_s[...]).astype(out_ref.dtype)

    pl.when(group < groups)(lambda: product(away_ref))
    pl.when(group >= groups)(lambda: product(kept_ref))


def grad_product(own, lhs, rhs):
    blocks = len(lhs)
    e = rhs[0][0].shape[-1]
    count = rhs[0][0].shape[0] if rhs[0][1] is None else 1
    groups = lhs[0].shape[1] // (2 * QB)

    def lhs_at(j, own):
        parity = jnp.where(j < groups, 1 - own[0], own[0])
        return (0, 2 * lax.rem(j, groups) + parity)

    def rhs_at(fixed):
        if fixed is None:
            return pl.BlockSpec((count, QB, e), lambda j, own: (0, 0, 0))
        return pl.BlockSpec((1, QB, e), lambda j, own: (fixed, 0, 0))

    out = jax.ShapeDtypeStruct((groups, count, e, QB), jnp.bfloat16)
    return pl.pallas_call(
        functools.partial(grad_kernel, blocks),
        grid_spec=pltpu.PrefetchScalarGridSpec(
            num_scalar_prefetch=1,
            grid=(2 * groups,),
            in_specs=[pl.BlockSpec((QB, QB), lhs_at)] * blocks
            + [rhs_at(fixed) for _, fixed in rhs],
            out_specs=[
                pl.BlockSpec(
                    (1, count, e, QB), lambda j, own: (jnp.minimum(j, groups - 1), 0, 0, 0)
                ),
                pl.BlockSpec((1, count, e, QB), lambda j, own: (jnp.maximum(j - groups, 0), 0, 0, 0)),
            ],
            scratch_shapes=[
                pltpu.VMEM((blocks * QB, QB), jnp.bfloat16),
                pltpu.VMEM((count * e, blocks * QB), jnp.bfloat16),
            ],
        ),
        out_shape=[out, out],
        compiler_params=pltpu.CompilerParams(vmem_limit_bytes=VMEM_LIMIT),
        cost_estimate=SMALL,
    )(own.reshape(1).astype(jnp.int32), *lhs, *[r for r, _ in rhs])


def turn_kernel(where_ref, a_ref, ra_ref, b_ref, rb_ref, out_ref):
    f32 = jnp.float32
    top = a_ref[0, 0].astype(f32) + ra_ref[0].astype(f32)
    bottom = b_ref[0, 0].astype(f32) + rb_ref[0].astype(f32)
    out_ref[0] = jnp.concatenate([top, bottom]).T


def turn(one, two, a, ra, b, rb):
    count, half, width = ra.shape
    part = pl.BlockSpec((1, half, width), lambda s, where: (s, 0, 0))
    return pl.pallas_call(
        turn_kernel,
        grid_spec=pltpu.PrefetchScalarGridSpec(
            num_scalar_prefetch=1,
            grid=(count,),
            in_specs=[
                pl.BlockSpec((1, 1, half, width), lambda s, where: (where[1], s, 0, 0)),
                part,
                pl.BlockSpec((1, 1, half, width), lambda s, where: (where[0], s, 0, 0)),
                part,
            ],
            out_specs=pl.BlockSpec((1, width, 2 * half), lambda s, where: (s, 0, 0)),
        ),
        out_shape=jax.ShapeDtypeStruct((count, width, 2 * half), jnp.float32),
        compiler_params=pltpu.CompilerParams(vmem_limit_bytes=VMEM_LIMIT),
        cost_estimate=SMALL,
    )(jnp.stack([one, two]).astype(jnp.int32), a, ra, b, rb)


def rows_kernel(blocks, *refs):
    w_ref, out_ref = refs[blocks], refs[blocks + 1]
    for k in range(blocks):
        out_ref[k * QB : (k + 1) * QB] = nn(refs[k][...], w_ref[...]).astype(out_ref.dtype)


def rows_product(lhs, w):
    blocks, inner, cols = len(lhs), w.shape[0], w.shape[1]
    wide = 512
    return pl.pallas_call(
        functools.partial(rows_kernel, blocks),
        grid=(cols // wide,),
        in_specs=[pl.BlockSpec((QB, inner), lambda n: (0, 0))] * blocks
        + [pl.BlockSpec((inner, wide), lambda n: (0, n))],
        out_specs=pl.BlockSpec((blocks * QB, wide), lambda n: (0, n)),
        out_shape=jax.ShapeDtypeStruct((blocks * QB, cols), jnp.bfloat16),
        compiler_params=pltpu.CompilerParams(vmem_limit_bytes=VMEM_LIMIT),
        cost_estimate=SMALL,
    )(*lhs, w)


class GradSum:
    def __init__(self, lhs, rhs):
        me = lax.axis_index("fsdp")
        self.low, self.one, self.two = me % 2, (me // 2) % 2, me // 4
        self.lhs, self.rhs = lhs, rhs
        self.staged = lax.axis_size("fsdp") == 8
        self.ra = self.rb = jnp.zeros((), jnp.bfloat16)

    def first(self, *others):
        own = self.low if self.staged else jnp.int32(1)
        self.away, self.kept = grad_product(after(own, *others), self.lhs, self.rhs)

    def ready(self):
        return [self.away, self.kept, self.ra, self.rb]

    def set(self, values):
        self.away, self.kept, self.ra, self.rb = values

    def exchange(self, one_step):
        if not self.staged:
            return
        if one_step == 0:
            self.back = send(self.away, flip(1), "fsdp")
        else:
            self.ra = send(self.ra, flip(2 * one_step), "fsdp")
            self.rb = send(self.rb, flip(4 // one_step), "fsdp")

    def part(self, index, axis, top, *more):
        groups, s, e, width = self.kept.shape
        start, size = [0] * 5, [2, 2, s, e // 2, width]
        start[axis], size[axis] = index, 1
        start[3] = 0 if top else e // 2
        total = 0.0
        for array in (self.kept, self.back):
            cut = lax.dynamic_slice(array.reshape(2, 2, s, e, width), start, size)
            total = total + jnp.squeeze(cut, axis).astype(jnp.float32)
        for array in more:
            total = total + array.astype(jnp.float32)
        return total.astype(jnp.bfloat16)

    def second(self, *others):
        if self.staged:
            self.kept, self.back = tie(self.kept, self.back, *others)[:2]
            self.ra = self.part(1 - self.one, 1, True)
            self.rb = self.part(1 - self.two, 0, False)

    def third(self, *others):
        if self.staged:
            ra, rb = tie(self.ra, self.rb, *others)[:2]
            self.a = self.part(self.one, 1, True, ra)
            self.b = self.part(self.two, 0, False, rb)
            self.ra = pick(self.a, 1 - self.two, 0)
            self.rb = pick(self.b, 1 - self.one, 0)

    def last(self, turned, *others):
        f32 = jnp.float32
        if not self.staged:
            both = jnp.stack([self.away, self.kept], axis=1)
            groups, _, s, e, width = both.shape
            both = both.transpose(2, 3, 0, 1, 4).reshape(s, e, 2 * groups * width)
            own = lax.psum_scatter(both, "fsdp", scatter_dimension=2, tiled=True).astype(f32)
            return own.transpose(0, 2, 1) if turned else own
        ra, rb = tie(self.ra, self.rb, *others)[:2]
        if turned:
            return turn(self.one, self.two, self.a, ra, self.b, rb)
        top = pick(self.a, self.two, 0).astype(f32) + ra.astype(f32)
        bottom = pick(self.b, self.one, 0).astype(f32) + rb.astype(f32)
        return jnp.concatenate([top, bottom], axis=1)


def per_device(layer_input, norm_gains, w_qkv, w_out, w_gate_up, w_down, doc_start, out_cotangent):
    bf, f32 = jnp.bfloat16, jnp.float32
    span_len = doc_start.shape[0]
    me = lax.axis_index("tp")
    mid = (me == 1) | (me == 2)
    per_seq = SEQ_LEN // span_len
    place = jnp.stack([lax.axis_index("fsdp") * span_len, me]).astype(jnp.int32)
    doc_row = doc_start.reshape(1, span_len)
    full_qkv = lax.all_gather(w_qkv, "fsdp", axis=1, tiled=True)
    full_out = lax.all_gather(w_out, "fsdp", axis=1, tiled=True)
    forth, back = neighbour_route(1, per_seq), neighbour_route(-1, per_seq)

    input_f32 = layer_input.astype(f32)
    unit_one, inverse_one = normalize(input_f32)
    normed_one = (unit_one * norm_gains[0]).astype(bf)
    x1, xm = tie(send(normed_one, PAIRS), send(normed_one, MIDDLE))
    xf, xo = tie(send(x1, MIDDLE), send(xm, OUTWARD))
    x2 = jnp.where(mid, xf, xo)
    x3 = send(xf, OUTWARD)
    cm = send(after(out_cotangent, xf), MIDDLE)
    full_qkv = after(full_qkv, xf)

    def project(block):
        return jnp.einsum("td,sde->ste", block, full_qkv, preferred_element_type=f32).astype(bf)

    attn_rows = [normed_one, x1, x2]
    new, old = [], []
    for block in attn_rows:
        new.append(project(block))
        old.append(send(new[-1][1:], forth, "fsdp"))
    tied = tie(x3, cm, *old)
    x3, cm, old = tied[0], tied[1], list(tied[2:])
    attn_rows.append(jnp.where(mid, xm, x3))
    new.append(project(attn_rows[3]))
    old.append(send(new[3][1:], forth, "fsdp"))
    old[3], w_gate_up, w_down = tie(old[3], w_gate_up, w_down)
    full_gate_up = lax.all_gather(w_gate_up, "fsdp", axis=1, tiled=True)
    full_down = lax.all_gather(w_down, "fsdp", axis=1, tiled=True)
    c1 = send(after(out_cotangent, new[3]), PAIRS)
    heads_out, lse = attend(place, doc_row, new, old)

    def out_part(k):
        return nn(heads_out[k * QB : (k + 1) * QB], full_out).astype(bf)

    a3 = out_part(3)
    t1 = send(a3, INWARD)
    c1, cm = tie(c1, after(cm, a3))
    cf, co = send(c1, MIDDLE), send(cm, OUTWARD)
    a2, a1, a0 = out_part(2), out_part(1), out_part(0)
    t1, cf, co, a2, a1, a0 = tie(t1, cf, co, a2, a1, a0)
    t2, t3 = send(a2, INWARD), send(add(a2, t1), MIDDLE)
    c3 = send(cf, OUTWARD)
    t2, t3, c3 = tie(t2, t3, c3)
    t4, t5 = send(add(a3, t2), MIDDLE), send(add(a1, t3), PAIRS)
    cot = [out_cotangent, c1, jnp.where(mid, cf, co), jnp.where(mid, cm, c3)]
    t4, t5 = tie(t4, t5)
    residual_mid = input_f32 + (a0.astype(f32) + t4.astype(f32) + t5.astype(f32))
    unit_two, inverse_two = normalize(residual_mid)
    normed_two = (unit_two * norm_gains[1]).astype(bf)

    def up(rows):
        return jnp.einsum("td,sdf->stf", rows, full_gate_up, preferred_element_type=f32)

    def down(gate_up, cot_rows):
        gate_pre, up_pre = gate_up[0], gate_up[1]
        sig = jax.nn.sigmoid(gate_pre)
        act = (gate_pre * sig * up_pre).astype(bf)
        grad_act = nt(cot_rows, full_down)
        grad_up = grad_act * gate_pre * sig
        grad_gate = grad_act * up_pre * sig * (1.0 + gate_pre * (1.0 - sig))
        grads = jnp.stack([grad_gate, grad_up]).astype(bf)
        back_part = jnp.einsum("stf,sdf->td", grads, full_gate_up, preferred_element_type=f32)
        return act, grads, back_part.astype(bf)

    m1, mm = send(normed_two, PAIRS), send(normed_two, MIDDLE)
    u0 = up(normed_two)
    m1, mm, u0 = tie(m1, mm, u0)
    mf, mo = send(m1, MIDDLE), send(mm, OUTWARD)
    u1 = up(m1)
    f0 = down(after(u0, u1), cot[0])
    mf, mo, u1, f0 = tie(mf, mo, u1, f0)
    m2 = jnp.where(mid, mf, mo)
    m3 = send(mf, OUTWARD)
    f1 = down(u1, cot[1])
    f2 = down(up(m2), cot[2])
    m3, f1, f2 = tie(m3, f1, f2)
    m3 = jnp.where(mid, mm, m3)
    f3 = down(up(m3), cot[3])
    g3, g2, g1, g0 = f3[2], f2[2], f1[2], f0[2]

    feed = (f0, f1, f2, f3)

    def join(sums, *values):
        count = len(values)
        tied = tie(*values, *[r for s in sums for r in s.ready()])
        for i, s in enumerate(sums):
            s.set(tied[count + 4 * i : count + 4 * i + 4])
        return tied[:count]

    t1 = send(g3, INWARD)
    mlp_rows = [normed_two, m1, m2, m3]
    up_sum = GradSum(mlp_rows, [(f[1], None) for f in feed])
    up_sum.first(g3)
    (t1,) = join([up_sum], t1)
    t2, t3 = send(after(g2, t1), INWARD), send(add(g2, t1), MIDDLE)
    up_sum.exchange(0)
    down_sum = GradSum(cot, [(f[0][None], None) for f in feed])
    down_sum.first(t1)
    down_part = rows_product([f[0] for f in feed[:3]] + [after(f3[0], t1)], full_down)
    t2, t3, down_part = join([down_sum], t2, t3, down_part)
    t4, t5 = send(add(g3, t2), MIDDLE), send(add(g1, t3), PAIRS)
    down_sum.exchange(0)
    up_sum.second(t2)
    t4, t5 = join([up_sum], t4, t5)
    grad_normed_two = g0.astype(f32) + t4.astype(f32) + t5.astype(f32)
    grad_mid = out_cotangent.astype(f32) + norm_back(
        grad_normed_two, norm_gains[1], unit_two, inverse_two
    )
    grad_branch = grad_mid.astype(bf)

    def heads_back(block):
        return nt(block, full_out).astype(bf)

    d3, d2, d1, d0 = [down_part[k * QB : (k + 1) * QB] for k in (3, 2, 1, 0)]
    b1, bm = send(grad_branch, PAIRS), send(grad_branch, MIDDLE)
    up_sum.exchange(1)
    down_sum.second(grad_branch)
    h0 = heads_back(grad_branch)
    b1, bm, h0 = join([down_sum], b1, bm, h0)
    bfar, bo = send(b1, MIDDLE), send(bm, OUTWARD)
    r1 = send(after(d3, b1), INWARD)
    h1 = heads_back(b1)
    up_sum.third(b1)
    bfar, bo, r1, h1 = join([up_sum], bfar, bo, r1, h1)
    b2 = jnp.where(mid, bfar, bo)
    b3 = send(bfar, OUTWARD)
    r2, r3 = send(after(d2, bfar), INWARD), send(add(d2, r1), MIDDLE)
    up_sum.exchange(2)
    down_sum.exchange(1)
    h2 = heads_back(b2)
    b3, r2, r3, h2 = tie(b3, r2, r3, h2)
    b3 = jnp.where(mid, bm, b3)
    h3 = heads_back(b3)
    r4, r5 = send(add(d3, r2), MIDDLE), send(add(d1, r3), PAIRS)
    cots = [h0, h1, h2, h3]
    half = heads_out.shape[1] // HEAD_DIM // 2
    *kept, prev_a = attend_back(place, doc_row, lse, new, old, cots, 0, half)
    n_a = send(prev_a, back, "fsdp")
    down_sum.third(prev_a)
    down_sum.exchange(2)
    *kept, prev_b = attend_back(place, doc_row, lse, new, old, cots, half, half, kept)
    n_b = send(prev_b, back, "fsdp")
    grad_q, own_k, own_v = kept
    head_blocks = heads_out.reshape(4, QB, -1)
    out_sum = GradSum([grad_branch, b1, b2, b3], [(head_blocks, k) for k in range(4)])
    out_sum.first(prev_b)
    up_own = up_sum.last(True, prev_b)
    n_a, n_b, r4, r5, up_own = join([out_sum], n_a, n_b, r4, r5, up_own)

    def piece(k):
        rows = slice(k * QB, (k + 1) * QB)
        arrived = jnp.concatenate([n_a[:, rows], n_b[:, rows]], axis=2)
        return jnp.stack([grad_q[rows], add(own_k[rows], arrived[0]), add(own_v[rows], arrived[1])])

    def first_back(grad):
        return jnp.einsum("ste,sde->td", grad, full_qkv, preferred_element_type=f32).astype(bf)

    q3 = piece(3)
    p3 = first_back(q3)
    t1 = send(p3, INWARD)
    out_sum.exchange(0)
    q2, q1, q0 = after(piece(2), p3), after(piece(1), p3), after(piece(0), p3)
    p2, p1, p0 = first_back(q2), first_back(q1), first_back(q0)
    qkv_sum = GradSum(attn_rows, [(q, None) for q in (q0, q1, q2, q3)])
    qkv_sum.first(p3)
    t1, p2, p1, p0 = join([qkv_sum], t1, p2, p1, p0)
    t2, t3 = send(p2, INWARD), send(add(p2, t1), MIDDLE)
    qkv_sum.exchange(0)
    gain_one = functools.reduce(
        jnp.add,
        [
            jnp.sum(p.astype(f32) * r.astype(f32), axis=0)
            for p, r in zip((p0, p1, p2, p3), attn_rows)
        ],
    )
    gain_two = jnp.sum(grad_normed_two * unit_two, axis=0)
    gains = jnp.stack([gain_one / norm_gains[0], gain_two])
    step = 1
    while step < lax.axis_size("fsdp"):
        gains = gains + send(gains, flip(step), "fsdp")
        step *= 2
    qkv_sum.second(t1)
    out_sum.second(t1)
    t2, t3, gains = join([qkv_sum, out_sum], t2, t3, gains)
    s1 = send(gains, INWARD)
    t4, t5 = send(add(p3, t2), MIDDLE), send(add(p1, t3), PAIRS)
    qkv_sum.exchange(1)
    out_sum.exchange(1)
    layer_output = (
        residual_mid + (d0.astype(f32) + r4.astype(f32) + after(r5, t2).astype(f32))
    ).astype(bf)
    down_own = down_sum.last(False, t2)
    gains = gains + s1
    s2 = send(gains, MIDDLE)
    qkv_sum.third(down_own)
    qkv_sum.exchange(2)
    out_sum.third(down_own)
    out_sum.exchange(2)
    gains = gains + s2
    s3 = send(gains, OUTWARD)
    grad_normed_one = p0.astype(f32) + t4.astype(f32) + t5.astype(f32)
    input_grad = (
        grad_mid + norm_back(grad_normed_one, norm_gains[0], unit_one, inverse_one)
    ).astype(bf)
    out_own = out_sum.last(False)
    qkv_own = qkv_sum.last(True)
    gains = jnp.where(mid, gains, s3)
    return (layer_output, input_grad, gains, qkv_own, out_own[0], up_own, down_own[0])


def solution(mesh):
    in_specs = (
        P(("fsdp", "tp"), None),
        P(),
        P(None, "fsdp", "tp"),
        P("tp", "fsdp"),
        P(None, "fsdp", "tp"),
        P("tp", "fsdp"),
        P("fsdp"),
        P(("fsdp", "tp"), None),
    )
    out_specs = (
        P(("fsdp", "tp"), None),
        P(("fsdp", "tp"), None),
        P(),
        P(None, "fsdp", "tp"),
        P("tp", "fsdp"),
        P(None, "fsdp", "tp"),
        P("tp", "fsdp"),
    )
    return jax.shard_map(
        per_device, mesh=mesh, in_specs=in_specs, out_specs=out_specs, check_vma=False
    )
```

```python
import functools
import math

import jax
import jax.numpy as jnp
from jax import lax
from jax.experimental import pallas as pl
from jax.experimental.pallas import tpu as pltpu
from jax.sharding import PartitionSpec as P

HEAD_DIM = 128
WINDOW = 1024
SEQ_LEN = 4096
QB = 256
SCALE = 1.0 / math.sqrt(HEAD_DIM)
LOG2E = 1.4426950408889634
EPS = 1e-06
MASKED = -1e30
VMEM_LIMIT = 36 << 20
ATTEND_LIMIT = 60 << 20
SMALL = pl.CostEstimate(flops=1 << 20, bytes_accessed=1 << 16, transcendentals=0)
NT = (((1,), (1,)), ((), ()))
TN = (((0,), (0,)), ((), ()))


def nt(a, b):
    return lax.dot_general(a, b, NT, preferred_element_type=jnp.float32)


def nn(a, b):
    return jnp.dot(a, b, preferred_element_type=jnp.float32)


def tn(a, b):
    return lax.dot_general(a, b, TN, preferred_element_type=jnp.float32)


def masked_scores(k_j, q, j, lo):
    s = nt(k_j, q)
    row = lax.broadcasted_iota(jnp.int32, s.shape, 0) + j * QB
    ok = row >= lo
    if (j + 1) * QB > WINDOW:
        hi = lax.broadcasted_iota(jnp.int32, (1, QB), 1) + WINDOW
        ok = ok & (row <= hi)
    return jnp.where(ok, s, MASKED)


def low_bound(doc_ref, b, off):
    q_row = lax.broadcasted_iota(jnp.int32, (1, QB), 1)
    doc = doc_ref[:, b * QB : (b + 1) * QB]
    return jnp.maximum(q_row + 1, doc - off + (WINDOW - b * QB))


def block_at(index):
    return pl.ds(pl.multiple_of(index * QB, QB), QB)


def attend_kernel(place_ref, doc_ref, *refs):
    new, old = refs[:4], refs[4:8]
    o_ref, lse_ref, q_s, k_s, vt_s = refs[8:]
    h = pl.program_id(0)
    off, me = place_ref[0], place_ref[1]
    blocks = len(new)
    for slot in range(blocks):
        at = me ^ slot
        q_s[block_at(at)] = new[slot][0]
        k_s[block_at(at)] = old[slot][0]
        k_s[block_at(at + blocks)] = new[slot][1]
        vt_s[:, block_at(at)] = old[slot][1].T
        vt_s[:, block_at(at + blocks)] = new[slot][2].T
    c = SCALE * LOG2E
    n = WINDOW // QB + 1
    for b in range(blocks):
        q = q_s[b * QB : (b + 1) * QB]
        lo = low_bound(doc_ref, b, off)
        ss = [
            masked_scores(k_s[(b + j) * QB : (b + j + 1) * QB], q, j, lo) for j in range(n)
        ]
        m = functools.reduce(jnp.maximum, [jnp.max(s, axis=0, keepdims=True) for s in ss])
        total = jnp.zeros((1, QB), jnp.float32)
        acc = jnp.zeros((HEAD_DIM, QB), jnp.float32)
        for j in range(n):
            p = jnp.exp2((ss[j] - m) * c)
            total = total + jnp.sum(p, axis=0, keepdims=True)
            acc = acc + nn(vt_s[:, (b + j) * QB : (b + j + 1) * QB], p.astype(jnp.bfloat16))
        o_ref[block_at(me ^ b)] = (acc / total).T.astype(o_ref.dtype)
        lse_ref[pl.ds(h, 1), b * QB : (b + 1) * QB] = m * c + jnp.log2(total)


def back_kernel(first, place_ref, doc_ref, lse_ref, *refs):
    new, old, cot = refs[:4], refs[4:8], refs[8:12]
    dq_ref, dk_ref, dv_ref, prev_ref, q_s, do_s, k_s, v_s, kt_s, dk_s, dv_s = refs[-11:]
    h = pl.program_id(0)
    off, me = place_ref[0], place_ref[1]
    blocks = len(new)
    for slot in range(blocks):
        at = me ^ slot
        q_s[block_at(at)] = new[slot][0]
        do_s[block_at(at)] = cot[slot][...]
        k_s[block_at(at)] = old[slot][0]
        k_s[block_at(at + blocks)] = new[slot][1]
        v_s[block_at(at)] = old[slot][1]
        v_s[block_at(at + blocks)] = new[slot][2]
        kt_s[:, block_at(at)] = old[slot][0].T
        kt_s[:, block_at(at + blocks)] = new[slot][1].T
    c = SCALE * LOG2E
    n = WINDOW // QB + 1
    seen = 0
    for b in range(blocks):
        q = q_s[b * QB : (b + 1) * QB]
        do = do_s[b * QB : (b + 1) * QB]
        lse = lse_ref[pl.ds(h + first, 1), b * QB : (b + 1) * QB]
        lo = low_bound(doc_ref, b, off)
        delta = jnp.zeros((1, QB), jnp.float32)
        ps, dps = [], []
        for j in range(n):
            rows = slice((b + j) * QB, (b + j + 1) * QB)
            p = jnp.exp2(masked_scores(k_s[rows], q, j, lo) * c - lse)
            dp = nt(v_s[rows], do)
            delta = delta + jnp.sum(p * dp, axis=0, keepdims=True)
            dv = nn(p.astype(jnp.bfloat16), do)
            if b + j >= seen:
                dv_s[rows] = dv
            else:
                dv_s[rows] += dv
            ps.append(p)
            dps.append(dp)
        dqt = jnp.zeros((HEAD_DIM, QB), jnp.float32)
        for j in range(n):
            rows = slice((b + j) * QB, (b + j + 1) * QB)
            ds = (ps[j] * (dps[j] - delta)).astype(jnp.bfloat16)
            dk = nn(ds, q)
            if b + j >= seen:
                dk_s[rows] = dk
            else:
                dk_s[rows] += dk
            dqt = dqt + nn(kt_s[:, rows], ds)
        seen = b + n
        dq_ref[block_at(me ^ b)] = (dqt * SCALE).T.astype(dq_ref.dtype)
    for slot in range(blocks):
        at = me ^ slot
        rows = slice(slot * QB, (slot + 1) * QB)
        prev_ref[0, rows] = (dk_s[block_at(at)] * SCALE).astype(prev_ref.dtype)
        prev_ref[1, rows] = dv_s[block_at(at)].astype(prev_ref.dtype)
        dk_ref[rows] = dk_s[block_at(at + blocks)] * SCALE
        dv_ref[rows] = dv_s[block_at(at + blocks)]


def spec2(rows, first=0):
    return pl.BlockSpec((rows, HEAD_DIM), lambda h: (0, h + first))


def spec3(count, rows, first=0):
    return pl.BlockSpec((count, rows, HEAD_DIM), lambda h: (0, 0, h + first))


def constant(shape):
    return pl.BlockSpec(shape, lambda h: (0, 0))


def attend(place, doc, new, old):
    blocks = len(new)
    span, width = blocks * QB, new[0].shape[-1]
    heads = width // HEAD_DIM
    bf = jnp.bfloat16
    return pl.pallas_call(
        attend_kernel,
        grid=(heads,),
        in_specs=[pl.BlockSpec(memory_space=pltpu.SMEM), constant((1, span))]
        + [spec3(3, QB)] * blocks
        + [spec3(2, QB)] * blocks,
        out_specs=[spec2(span), constant((heads, span))],
        out_shape=[
            jax.ShapeDtypeStruct((span, width), bf),
            jax.ShapeDtypeStruct((heads, span), jnp.float32),
        ],
        scratch_shapes=[
            pltpu.VMEM((span, HEAD_DIM), bf),
            pltpu.VMEM((WINDOW + span, HEAD_DIM), bf),
            pltpu.VMEM((HEAD_DIM, WINDOW + span), bf),
        ],
        compiler_params=pltpu.CompilerParams(vmem_limit_bytes=ATTEND_LIMIT),
        cost_estimate=SMALL,
    )(place, doc, *new, *old)


def attend_back(place, doc, lse, new, old, cot, first, heads, kept=()):
    blocks = len(new)
    span, width = blocks * QB, new[0].shape[-1]
    bf, f32 = jnp.bfloat16, jnp.float32
    fixed = 3 + 3 * blocks
    return pl.pallas_call(
        functools.partial(back_kernel, first),
        grid=(heads,),
        in_specs=[
            pl.BlockSpec(memory_space=pltpu.SMEM),
            constant((1, span)),
            constant(lse.shape),
        ]
        + [spec3(3, QB, first)] * blocks
        + [spec3(2, QB, first)] * blocks
        + [spec2(QB, first)] * blocks
        + [pl.BlockSpec(memory_space=pl.ANY)] * len(kept),
        out_specs=[spec2(span, first)] * 3 + [spec3(2, WINDOW)],
        out_shape=[
            jax.ShapeDtypeStruct((span, width), bf),
            jax.ShapeDtypeStruct((span, width), f32),
            jax.ShapeDtypeStruct((span, width), f32),
            jax.ShapeDtypeStruct((2, WINDOW, heads * HEAD_DIM), bf),
        ],
        input_output_aliases={fixed + i: i for i in range(len(kept))},
        scratch_shapes=[pltpu.VMEM((span, HEAD_DIM), bf)] * 2
        + [pltpu.VMEM((WINDOW + span, HEAD_DIM), bf)] * 2
        + [pltpu.VMEM((HEAD_DIM, WINDOW + span), bf)]
        + [pltpu.VMEM((WINDOW + span, HEAD_DIM), f32)] * 2,
        compiler_params=pltpu.CompilerParams(vmem_limit_bytes=ATTEND_LIMIT),
        cost_estimate=SMALL,
    )(place, doc, lse, *new, *old, *cot, *kept)


PAIRS = [(0, 1), (1, 0), (2, 3), (3, 2)]
MIDDLE = [(1, 2), (2, 1)]
OUTWARD = [(1, 0), (2, 3)]
INWARD = [(0, 1), (3, 2)]


def send(block, route, axis="tp"):
    return lax.ppermute(block, axis, route)


def tie(*values):
    return lax.optimization_barrier(values)


def after(value, *others):
    return lax.optimization_barrier((value,) + others)[0]


def flip(bit, axis="fsdp"):
    return [(i, i ^ bit) for i in range(lax.axis_size(axis))]


def neighbour_route(distance, per_seq):
    size = lax.axis_size("fsdp")
    pairs = [(i - 1, i) for i in range(1, size) if i % per_seq]
    return pairs if distance > 0 else [(b, a) for a, b in pairs]


def pick(array, index, axis):
    return lax.dynamic_index_in_dim(array, index, axis, keepdims=False)


NORM_ROWS = 64


def row_mean(values):
    return jnp.mean(values, axis=-1, keepdims=True)


def total_of(first, *more):
    total = first.astype(jnp.float32)
    for array in more:
        total = total + array.astype(jnp.float32)
    return total


def norm_kernel(parts, gain_ref, *refs):
    total = total_of(*[ref[...] for ref in refs[:parts]])
    inverse = lax.rsqrt(row_mean(total * total) + EPS)
    refs[parts][...] = (total * inverse * gain_ref[...]).astype(jnp.bfloat16)
    refs[parts + 1][...] = jnp.broadcast_to(inverse, refs[parts + 1].shape)
    if len(refs) > parts + 2:
        refs[parts + 2][...] = total


def row_call(kernel, gain, arrays, outs, sums=0):
    rows, width = arrays[0].shape
    block = lambda w: pl.BlockSpec((NORM_ROWS, w), lambda r: (r, 0))
    one = pl.BlockSpec((1, width), lambda r: (0, 0))
    return pl.pallas_call(
        kernel,
        grid=(rows // NORM_ROWS,),
        in_specs=[one] + [block(a.shape[1]) for a in arrays],
        out_specs=[block(w) for w, _ in outs] + [one] * sums,
        out_shape=[jax.ShapeDtypeStruct((rows, w), t) for w, t in outs]
        + [jax.ShapeDtypeStruct((1, width), jnp.float32)] * sums,
        compiler_params=pltpu.CompilerParams(vmem_limit_bytes=VMEM_LIMIT),
        cost_estimate=SMALL,
    )(gain[None], *arrays)


def norm(gain, parts, keep):
    width = parts[0].shape[1]
    outs = [(width, jnp.bfloat16), (128, jnp.float32)] + [(width, jnp.float32)] * keep
    return row_call(functools.partial(norm_kernel, len(parts)), gain, parts, outs)


def norm_back_kernel(parts, gain_ref, *refs):
    grad = total_of(*[ref[...] for ref in refs[:parts]])
    value_ref, inverse_ref, more_ref = refs[parts : parts + 3]
    outs = refs[parts + 3 :]
    inverse = inverse_ref[:, :1]
    unit = value_ref[...].astype(jnp.float32) * inverse
    scaled = grad * gain_ref[...]
    result = more_ref[...].astype(jnp.float32) + inverse * (
        scaled - unit * row_mean(scaled * unit)
    )
    outs[0][...] = result.astype(jnp.bfloat16)
    if len(outs) == 3:
        outs[1][...] = result

        @pl.when(pl.program_id(0) == 0)
        def _():
            outs[2][...] = jnp.zeros_like(outs[2])

        outs[2][...] += jnp.sum(grad * unit, axis=0, keepdims=True)


def norm_back(gain, parts, value, inverse, more, keep):
    width = value.shape[1]
    outs = [(width, jnp.bfloat16)] + [(width, jnp.float32)] * keep
    return row_call(
        functools.partial(norm_back_kernel, len(parts)),
        gain,
        [*parts, value, inverse, more],
        outs,
        sums=int(keep),
    )


def add(a, b):
    return (a.astype(jnp.float32) + b.astype(jnp.float32)).astype(jnp.bfloat16)


def grad_kernel(blocks, which_ref, *refs):
    lhs, rhs = refs[:blocks], refs[blocks : 2 * blocks]
    away_ref, kept_ref, lhs_s, rhs_s = refs[2 * blocks :]
    count, e = away_ref.shape[1:3]
    group, groups = pl.program_id(0), pl.num_programs(0) // 2

    @pl.when(group == 0)
    def _():
        for k in range(blocks):
            for s in range(count):
                rhs_s[s * e : (s + 1) * e, k * QB : (k + 1) * QB] = rhs[k][s].T

    for k in range(blocks):
        lhs_s[k * QB : (k + 1) * QB] = lhs[k][...]

    def product(out_ref):
        for s in range(count):
            out_ref[0, s] = nn(rhs_s[s * e : (s + 1) * e], lhs_s[...]).astype(out_ref.dtype)

    pl.when(group < groups)(lambda: product(away_ref))
    pl.when(group >= groups)(lambda: product(kept_ref))


def grad_product(own, lhs, rhs):
    blocks = len(lhs)
    e = rhs[0][0].shape[-1]
    count = rhs[0][1]
    groups = lhs[0].shape[1] // (2 * QB)

    def lhs_at(j, own):
        parity = jnp.where(j < groups, 1 - own[0], own[0])
        return (0, 2 * lax.rem(j, groups) + parity)

    def rhs_at(array, k):
        at = (0, k, 0) if array.shape[0] == count else (k, 0, 0)
        return pl.BlockSpec((count, QB, e), lambda j, own: at)

    out = jax.ShapeDtypeStruct((groups, count, e, QB), jnp.bfloat16)
    return pl.pallas_call(
        functools.partial(grad_kernel, blocks),
        grid_spec=pltpu.PrefetchScalarGridSpec(
            num_scalar_prefetch=1,
            grid=(2 * groups,),
            in_specs=[pl.BlockSpec((QB, QB), lhs_at)] * blocks
            + [rhs_at(array, k) for array, _, k in rhs],
            out_specs=[
                pl.BlockSpec(
                    (1, count, e, QB), lambda j, own: (jnp.minimum(j, groups - 1), 0, 0, 0)
                ),
                pl.BlockSpec((1, count, e, QB), lambda j, own: (jnp.maximum(j - groups, 0), 0, 0, 0)),
            ],
            scratch_shapes=[
                pltpu.VMEM((blocks * QB, QB), jnp.bfloat16),
                pltpu.VMEM((count * e, blocks * QB), jnp.bfloat16),
            ],
        ),
        out_shape=[out, out],
        compiler_params=pltpu.CompilerParams(vmem_limit_bytes=VMEM_LIMIT),
        cost_estimate=SMALL,
    )(own.reshape(1).astype(jnp.int32), *lhs, *[r[0] for r in rhs])


def turn_kernel(group_ref, kept_ref, back_ref, *refs):
    total = kept_ref[0, 0].astype(jnp.float32) + back_ref[0, 0].astype(jnp.float32)
    for ref in refs[:-1]:
        total = total + ref[0].astype(jnp.float32)
    refs[-1][0] = total.T


def turn(group, kept, back, parts):
    groups, count, e, width = kept.shape
    mine = pl.BlockSpec((1, 1, e, width), lambda s, group: (group[0], s, 0, 0))
    return pl.pallas_call(
        turn_kernel,
        grid_spec=pltpu.PrefetchScalarGridSpec(
            num_scalar_prefetch=1,
            grid=(count,),
            in_specs=[mine, mine]
            + [pl.BlockSpec((1, e, width), lambda s, group: (s, 0, 0))] * len(parts),
            out_specs=pl.BlockSpec((1, width, e), lambda s, group: (s, 0, 0)),
        ),
        out_shape=jax.ShapeDtypeStruct((count, width, e), jnp.float32),
        compiler_params=pltpu.CompilerParams(vmem_limit_bytes=VMEM_LIMIT),
        cost_estimate=SMALL,
    )(group.reshape(1).astype(jnp.int32), kept, back, *parts)


def rows_kernel(blocks, *refs):
    w_ref, out_ref = refs[blocks], refs[blocks + 1]
    for k in range(blocks):
        out_ref[k * QB : (k + 1) * QB] = nn(refs[k][...], w_ref[...]).astype(out_ref.dtype)


def rows_product(lhs, w):
    blocks, inner, cols = len(lhs), w.shape[0], w.shape[1]
    wide = 512
    return pl.pallas_call(
        functools.partial(rows_kernel, blocks),
        grid=(cols // wide,),
        in_specs=[pl.BlockSpec((QB, inner), lambda n: (0, 0))] * blocks
        + [pl.BlockSpec((inner, wide), lambda n: (0, n))],
        out_specs=pl.BlockSpec((blocks * QB, wide), lambda n: (0, n)),
        out_shape=jax.ShapeDtypeStruct((blocks * QB, cols), jnp.bfloat16),
        compiler_params=pltpu.CompilerParams(vmem_limit_bytes=VMEM_LIMIT),
        cost_estimate=SMALL,
    )(*lhs, w)


class GradSum:
    def __init__(self, lhs, rhs, direct):
        me = lax.axis_index("fsdp")
        self.low, self.one, self.two = me % 2, (me // 2) % 2, me // 4
        self.group = me // 2
        self.lhs, self.rhs, self.direct = lhs, rhs, direct
        self.staged = lax.axis_size("fsdp") == 8
        self.back, self.parts = jnp.zeros((), jnp.bfloat16), []

    def product(self, *others):
        own = self.low if self.staged else jnp.int32(1)
        self.away, self.kept = grad_product(after(own, *others), self.lhs, self.rhs)

    def swap(self):
        if self.staged:
            self.back = send(self.away, flip(1), "fsdp")

    def half(self, index, axis, top, *more):
        groups, s, e, width = self.kept.shape
        start, size = [0] * 5, [2, 2, s, e // 2, width]
        start[axis], size[axis] = index, 1
        start[3] = 0 if top else e // 2
        cuts = [
            jnp.squeeze(lax.dynamic_slice(a.reshape(2, 2, s, e, width), start, size), axis)
            for a in (self.kept, self.back)
        ]
        return total_of(*cuts, *more).astype(jnp.bfloat16)

    def split(self):
        if self.staged and self.direct:
            self.parts = [
                total_of(pick(self.kept, self.group ^ k, 0), pick(self.back, self.group ^ k, 0))
                for k in (1, 2, 3)
            ]
            self.parts = [part.astype(jnp.bfloat16) for part in self.parts]
        elif self.staged:
            self.parts = [self.half(1 - self.one, 1, True), self.half(1 - self.two, 0, False)]

    def spread(self):
        routes = (2, 4, 6) if self.direct else (2, 4)
        self.parts = [send(p, flip(r), "fsdp") for p, r in zip(self.parts, routes)]

    def refine(self):
        if self.staged:
            self.a = self.half(self.one, 1, True, self.parts[0])
            self.b = self.half(self.two, 0, False, self.parts[1])
            self.parts = [pick(self.a, 1 - self.two, 0), pick(self.b, 1 - self.one, 0)]

    def finish(self):
        self.parts = [send(p, flip(r), "fsdp") for p, r in zip(self.parts, (4, 2))]

    def own(self, turned, *others):
        if not self.staged:
            both = jnp.stack([self.away, self.kept], axis=1)
            groups, _, s, e, width = both.shape
            both = both.transpose(2, 3, 0, 1, 4).reshape(s, e, 2 * groups * width)
            own = lax.psum_scatter(both, "fsdp", scatter_dimension=2, tiled=True)
            own = own.astype(jnp.float32)
            return own.transpose(0, 2, 1) if turned else own
        parts = tie(*self.parts, *others)[: len(self.parts)]
        if not self.direct:
            top = total_of(pick(self.a, self.two, 0), parts[0])
            bottom = total_of(pick(self.b, self.one, 0), parts[1])
            own = jnp.concatenate([top, bottom], axis=1)
            return own.transpose(0, 2, 1) if turned else own
        if turned:
            return turn(self.group, self.kept, self.back, parts)
        return total_of(pick(self.kept, self.group, 0), pick(self.back, self.group, 0), *parts)


def join(sums, *values):
    held = [[s.away, s.kept, s.back, *s.parts] for s in sums]
    tied = list(tie(*values, *[h for hs in held for h in hs]))
    out, tied = tied[: len(values)], tied[len(values) :]
    for s, hs in zip(sums, held):
        s.away, s.kept, s.back, *s.parts = tied[: len(hs)]
        tied = tied[len(hs) :]
    return out


def per_device(layer_input, norm_gains, w_qkv, w_out, w_gate_up, w_down, doc_start, out_cotangent):
    bf, f32 = jnp.bfloat16, jnp.float32
    span_len = doc_start.shape[0]
    me = lax.axis_index("tp")
    mid = (me == 1) | (me == 2)
    per_seq = SEQ_LEN // span_len
    place = jnp.stack([lax.axis_index("fsdp") * span_len, me]).astype(jnp.int32)
    doc_row = doc_start.reshape(1, span_len)
    full_qkv = lax.all_gather(w_qkv, "fsdp", axis=1, tiled=True)
    full_out = lax.all_gather(w_out, "fsdp", axis=1, tiled=True)
    forth, back = neighbour_route(1, per_seq), neighbour_route(-1, per_seq)

    normed_one, inverse_one = norm(norm_gains[0], [layer_input], False)
    xm, x1 = send(normed_one, MIDDLE), send(normed_one, PAIRS)
    xo, xf = send(xm, OUTWARD), send(x1, MIDDLE)
    full_qkv = after(full_qkv, x1)

    def project(block):
        return jnp.einsum("td,sde->ste", block, full_qkv, preferred_element_type=f32).astype(bf)

    first = project(normed_one)
    xf, xo, first = tie(xf, xo, first)
    x2 = jnp.where(mid, xf, xo)
    x3 = send(xf, OUTWARD)
    attn_rows = [normed_one, x1, x2]
    new = [first, project(x1), project(x2)]
    old = [send(n[1:], forth, "fsdp") for n in new]
    x3, *old = tie(x3, *old)
    attn_rows.append(jnp.where(mid, xm, x3))
    new.append(project(attn_rows[3]))
    old.append(send(new[3][1:], forth, "fsdp"))
    old[3], w_gate_up, w_down = tie(old[3], w_gate_up, w_down)
    full_gate_up = lax.all_gather(w_gate_up, "fsdp", axis=1, tiled=True)
    full_down = lax.all_gather(w_down, "fsdp", axis=1, tiled=True)
    late_cot = after(out_cotangent, new[3])
    c1, cm = send(late_cot, PAIRS), send(late_cot, MIDDLE)
    heads_out, lse = attend(place, doc_row, new, old)

    def out_part(k):
        return nn(heads_out[k * QB : (k + 1) * QB], full_out).astype(bf)

    def cross(middle, end):
        return send(jnp.where(mid, middle, end), PAIRS)

    a3 = out_part(3)
    y1 = cross(after(cm, a3), a3)
    c1 = after(c1, a3)
    cf = send(c1, MIDDLE)
    a2, a1, a0 = out_part(2), out_part(1), out_part(0)
    y1, cf, a2, a1, a0 = tie(y1, cf, a2, a1, a0)
    y2, t3 = cross(cf, a2), send(add(a2, y1), MIDDLE)
    y2, t3 = tie(y2, t3)
    t4, t5 = send(add(a3, y2), MIDDLE), send(add(a1, t3), PAIRS)
    cot = [out_cotangent, c1, jnp.where(mid, cf, y1), jnp.where(mid, cm, y2)]
    t4, t5 = tie(t4, t5)
    normed_two, inverse_two, residual_mid = norm(norm_gains[1], [layer_input, a0, t4, t5], True)

    def up(rows):
        return jnp.einsum("td,sdf->stf", rows, full_gate_up, preferred_element_type=f32)

    def down(gate_up, cot_rows):
        gate_pre, up_pre = gate_up[0], gate_up[1]
        sig = jax.nn.sigmoid(gate_pre)
        act = (gate_pre * sig * up_pre).astype(bf)
        grad_act = nt(cot_rows, full_down)
        grad_up = grad_act * gate_pre * sig
        grad_gate = grad_act * up_pre * sig * (1.0 + gate_pre * (1.0 - sig))
        return act, jnp.stack([grad_gate, grad_up]).astype(bf)

    def second_back(grads):
        return jnp.einsum("stf,sdf->td", grads, full_gate_up, preferred_element_type=f32).astype(bf)

    m1, mm = send(normed_two, PAIRS), send(normed_two, MIDDLE)
    u0 = up(normed_two)
    m1, mm, u0 = tie(m1, mm, u0)
    mo, mf = send(mm, OUTWARD), send(m1, MIDDLE)
    u1 = up(m1)
    f0 = down(after(u0, u1), cot[0])
    mf, mo, u1, f0 = tie(mf, mo, u1, f0)
    m2 = jnp.where(mid, mf, mo)
    m3 = send(mf, OUTWARD)
    f1 = down(u1, cot[1])
    f2 = down(up(m2), cot[2])
    g0, g1, g2 = second_back(f0[1]), second_back(f1[1]), second_back(f2[1])
    m3, f1, f2, g0, g1, g2 = tie(m3, f1, f2, g0, g1, g2)
    m3 = jnp.where(mid, mm, m3)
    f3 = down(up(m3), cot[3])
    g3 = second_back(f3[1])

    feed = (f0, f1, f2, f3)
    t1 = send(g3, INWARD)
    up_sum = GradSum([normed_two, m1, m2, m3], [(f[1], 2, 0) for f in feed], False)
    up_sum.product(g3)
    (t1,) = join([up_sum], t1)
    t2, t3 = send(after(g2, t1), INWARD), send(add(g2, t1), MIDDLE)
    up_sum.swap()
    down_sum = GradSum(cot, [(f[0][None], 1, 0) for f in feed], False)
    down_sum.product(t1)
    t2, t3 = join([up_sum, down_sum], t2, t3)
    t4, t5 = send(add(g3, t2), MIDDLE), send(add(g1, t3), PAIRS)
    down_sum.swap()
    up_sum.split()
    down_part = rows_product([f[0] for f in feed[:3]] + [after(f3[0], t2)], full_down)
    t4, t5, down_part = join([up_sum, down_sum], t4, t5, down_part)
    grad_branch, grad_mid, gain_two = norm_back(
        norm_gains[1], [g0, t4, t5], residual_mid, inverse_two, out_cotangent, True
    )

    def heads_back(block):
        return nt(block, full_out).astype(bf)

    d3, d2, d1, d0 = [down_part[k * QB : (k + 1) * QB] for k in (3, 2, 1, 0)]
    b1, bm = send(grad_branch, PAIRS), send(grad_branch, MIDDLE)
    up_sum.spread()
    down_sum.kept = after(down_sum.kept, grad_branch)
    down_sum.split()
    h0 = heads_back(grad_branch)
    b1, bm, h0 = join([down_sum], b1, bm, h0)
    y1, bfar = cross(bm, d3), send(b1, MIDDLE)
    down_sum.spread()
    h1 = heads_back(b1)
    y1, bfar, h1 = join([up_sum], y1, bfar, h1)
    b2 = jnp.where(mid, bfar, y1)
    y2, r3 = cross(bfar, d2), send(add(d2, y1), MIDDLE)
    up_sum.refine()
    h2 = heads_back(b2)
    y2, r3, h2 = join([up_sum, down_sum], y2, r3, h2)
    b3 = jnp.where(mid, bm, y2)
    h3 = heads_back(b3)
    r4, r5 = send(add(d3, y2), MIDDLE), send(add(d1, r3), PAIRS)
    up_sum.finish()
    cots = [h0, h1, h2, h3]
    half = heads_out.shape[1] // HEAD_DIM // 2
    *kept, prev_a = attend_back(place, doc_row, lse, new, old, cots, 0, half)
    head_blocks = heads_out.reshape(4, QB, -1)
    gb_blocks = [grad_branch, b1, b2, b3]
    out_sum = GradSum(gb_blocks, [(head_blocks, 1, k) for k in range(4)], True)
    out_sum.product(h3)
    r4, r5, prev_a, *kept = join([out_sum, up_sum, down_sum], r4, r5, prev_a, *kept)
    n_a = send(prev_a, back, "fsdp")
    out_sum.swap()
    *kept, prev_b = attend_back(place, doc_row, lse, new, old, cots, half, half, kept)
    n_a, prev_b, *kept = join([out_sum, down_sum], n_a, prev_b, *kept)
    n_b = send(prev_b, back, "fsdp")
    grad_q, own_k, own_v = kept
    out_sum.split()
    down_sum.refine()
    up_own = up_sum.own(True, prev_b)
    n_b, up_own = join([out_sum, down_sum], n_b, up_own)

    def piece(rows):
        arrived = jnp.concatenate([n_a[:, rows], n_b[:, rows]], axis=2)
        return jnp.stack([grad_q[rows], add(own_k[rows], arrived[0]), add(own_v[rows], arrived[1])])

    def first_back(grad):
        return jnp.einsum("ste,sde->td", grad, full_qkv, preferred_element_type=f32).astype(bf)

    last = slice(3 * QB, 4 * QB)
    q3 = piece(last)
    p3 = first_back(q3)
    t1 = send(p3, INWARD)
    out_sum.spread()
    down_sum.finish()
    q012 = after(piece(slice(0, 3 * QB)), p3)
    p012 = first_back(q012)
    qkv_sum = GradSum(attn_rows, [(q012, 3, k) for k in range(3)] + [(q3, 3, 0)], True)
    qkv_sum.product(p3)
    t1, p012, p3 = join([qkv_sum, out_sum, down_sum], t1, p012, p3)
    p0, p1, p2 = [p012[k * QB : (k + 1) * QB] for k in range(3)]
    t2, t3 = send(p2, INWARD), send(add(p2, t1), MIDDLE)
    qkv_sum.swap()
    qkv_sum.split()
    qkv_sum.spread()
    late = tie(p0, p1, p2, p3, qkv_sum.back)[:4]
    gain_one = functools.reduce(
        jnp.add,
        [jnp.sum(p.astype(f32) * r.astype(f32), axis=0) for p, r in zip(late, attn_rows)],
    )
    gains = jnp.stack([gain_one / norm_gains[0], gain_two[0]])
    if lax.axis_size("fsdp") == 8:
        gains = [gains] + [send(gains, flip(k), "fsdp") for k in range(1, 8)]
    else:
        gains = [lax.psum(gains, "fsdp")]
    down_own = down_sum.own(False)
    t2, t3, down_own, *gains = tie(t2, t3, down_own, *gains)
    t4, t5 = send(add(p3, t2), MIDDLE), send(add(p1, t3), PAIRS)
    gains = total_of(*gains)
    out_own = out_sum.own(False, t2)
    layer_output = (
        residual_mid + (d0.astype(f32) + r4.astype(f32) + after(r5, t2).astype(f32))
    ).astype(bf)
    t4, t5, gains, layer_output, out_own = tie(t4, t5, gains, layer_output, out_own)
    gains = total_of(gains, *[send(gains, flip(k, "tp"), "tp") for k in (1, 2, 3)])
    (input_grad,) = norm_back(
        norm_gains[0], [p0, t4, t5], layer_input, inverse_one, grad_mid, False
    )
    qkv_own = qkv_sum.own(True, t5)
    return (layer_output, input_grad, gains, qkv_own, out_own[0], up_own, down_own[0])


def solution(mesh):
    in_specs = (
        P(("fsdp", "tp"), None),
        P(),
        P(None, "fsdp", "tp"),
        P("tp", "fsdp"),
        P(None, "fsdp", "tp"),
        P("tp", "fsdp"),
        P("fsdp"),
        P(("fsdp", "tp"), None),
    )
    out_specs = (
        P(("fsdp", "tp"), None),
        P(("fsdp", "tp"), None),
        P(),
        P(None, "fsdp", "tp"),
        P("tp", "fsdp"),
        P(None, "fsdp", "tp"),
        P("tp", "fsdp"),
    )
    return jax.shard_map(
        per_device, mesh=mesh, in_specs=in_specs, out_specs=out_specs, check_vma=False
    )
```

```python
import functools
import math

import jax
import jax.numpy as jnp
from jax import lax
from jax.experimental import pallas as pl
from jax.experimental.pallas import tpu as pltpu
from jax.sharding import PartitionSpec as P

HEAD_DIM = 128
WINDOW = 1024
SEQ_LEN = 4096
QB = 256
SCALE = 1.0 / math.sqrt(HEAD_DIM)
LOG2E = 1.4426950408889634
EPS = 1e-06
MASKED = -1e30
VMEM_LIMIT = 36 << 20
ATTEND_LIMIT = 60 << 20
SMALL = pl.CostEstimate(flops=1 << 20, bytes_accessed=1 << 16, transcendentals=0)
NT = (((1,), (1,)), ((), ()))
TN = (((0,), (0,)), ((), ()))


def nt(a, b):
    return lax.dot_general(a, b, NT, preferred_element_type=jnp.float32)


def nn(a, b):
    return jnp.dot(a, b, preferred_element_type=jnp.float32)


def tn(a, b):
    return lax.dot_general(a, b, TN, preferred_element_type=jnp.float32)


def masked_scores(k_j, q, j, lo):
    s = nt(k_j, q)
    row = lax.broadcasted_iota(jnp.int32, s.shape, 0) + j * QB
    ok = row >= lo
    if (j + 1) * QB > WINDOW:
        hi = lax.broadcasted_iota(jnp.int32, (1, QB), 1) + WINDOW
        ok = ok & (row <= hi)
    return jnp.where(ok, s, MASKED)


def low_bound(doc_ref, b, off):
    q_row = lax.broadcasted_iota(jnp.int32, (1, QB), 1)
    doc = doc_ref[:, b * QB : (b + 1) * QB]
    return jnp.maximum(q_row + 1, doc - off + (WINDOW - b * QB))


def block_at(index):
    return pl.ds(pl.multiple_of(index * QB, QB), QB)


def attend_kernel(place_ref, doc_ref, *refs):
    new, old = refs[:4], refs[4:8]
    o_ref, lse_ref, q_s, k_s, vt_s = refs[8:]
    h = pl.program_id(0)
    off, me = place_ref[0], place_ref[1]
    blocks = len(new)
    for slot in range(blocks):
        at = me ^ slot
        q_s[block_at(at)] = new[slot][0]
        k_s[block_at(at)] = old[slot][0]
        k_s[block_at(at + blocks)] = new[slot][1]
        vt_s[:, block_at(at)] = old[slot][1].T
        vt_s[:, block_at(at + blocks)] = new[slot][2].T
    c = SCALE * LOG2E
    n = WINDOW // QB + 1
    for b in range(blocks):
        q = q_s[b * QB : (b + 1) * QB]
        lo = low_bound(doc_ref, b, off)
        ss = [
            masked_scores(k_s[(b + j) * QB : (b + j + 1) * QB], q, j, lo) for j in range(n)
        ]
        m = functools.reduce(jnp.maximum, [jnp.max(s, axis=0, keepdims=True) for s in ss])
        total = jnp.zeros((1, QB), jnp.float32)
        acc = jnp.zeros((HEAD_DIM, QB), jnp.float32)
        for j in range(n):
            p = jnp.exp2((ss[j] - m) * c)
            total = total + jnp.sum(p, axis=0, keepdims=True)
            acc = acc + nn(vt_s[:, (b + j) * QB : (b + j + 1) * QB], p.astype(jnp.bfloat16))
        o_ref[block_at(me ^ b)] = (acc / total).T.astype(o_ref.dtype)
        lse_ref[pl.ds(h, 1), b * QB : (b + 1) * QB] = m * c + jnp.log2(total)


def back_kernel(first, place_ref, doc_ref, lse_ref, *refs):
    new, old, cot = refs[:4], refs[4:8], refs[8:12]
    dq_ref, dk_ref, dv_ref, prev_ref, q_s, do_s, k_s, v_s, kt_s, dk_s, dv_s = refs[-11:]
    h = pl.program_id(0)
    off, me = place_ref[0], place_ref[1]
    blocks = len(new)
    for slot in range(blocks):
        at = me ^ slot
        q_s[block_at(at)] = new[slot][0]
        do_s[block_at(at)] = cot[slot][...]
        k_s[block_at(at)] = old[slot][0]
        k_s[block_at(at + blocks)] = new[slot][1]
        v_s[block_at(at)] = old[slot][1]
        v_s[block_at(at + blocks)] = new[slot][2]
        kt_s[:, block_at(at)] = old[slot][0].T
        kt_s[:, block_at(at + blocks)] = new[slot][1].T
    c = SCALE * LOG2E
    n = WINDOW // QB + 1
    seen = 0
    for b in range(blocks):
        q = q_s[b * QB : (b + 1) * QB]
        do = do_s[b * QB : (b + 1) * QB]
        lse = lse_ref[pl.ds(h + first, 1), b * QB : (b + 1) * QB]
        lo = low_bound(doc_ref, b, off)
        delta = jnp.zeros((1, QB), jnp.float32)
        ps, dps = [], []
        for j in range(n):
            rows = slice((b + j) * QB, (b + j + 1) * QB)
            p = jnp.exp2(masked_scores(k_s[rows], q, j, lo) * c - lse)
            dp = nt(v_s[rows], do)
            delta = delta + jnp.sum(p * dp, axis=0, keepdims=True)
            dv = nn(p.astype(jnp.bfloat16), do)
            if b + j >= seen:
                dv_s[rows] = dv
            else:
                dv_s[rows] += dv
            ps.append(p)
            dps.append(dp)
        dqt = jnp.zeros((HEAD_DIM, QB), jnp.float32)
        for j in range(n):
            rows = slice((b + j) * QB, (b + j + 1) * QB)
            ds = (ps[j] * (dps[j] - delta)).astype(jnp.bfloat16)
            dk = nn(ds, q)
            if b + j >= seen:
                dk_s[rows] = dk
            else:
                dk_s[rows] += dk
            dqt = dqt + nn(kt_s[:, rows], ds)
        seen = b + n
        dq_ref[block_at(me ^ b)] = (dqt * SCALE).T.astype(dq_ref.dtype)
    for slot in range(blocks):
        at = me ^ slot
        rows = slice(slot * QB, (slot + 1) * QB)
        prev_ref[0, rows] = (dk_s[block_at(at)] * SCALE).astype(prev_ref.dtype)
        prev_ref[1, rows] = dv_s[block_at(at)].astype(prev_ref.dtype)
        dk_ref[rows] = dk_s[block_at(at + blocks)] * SCALE
        dv_ref[rows] = dv_s[block_at(at + blocks)]


def spec2(rows, first=0):
    return pl.BlockSpec((rows, HEAD_DIM), lambda h: (0, h + first))


def spec3(count, rows, first=0):
    return pl.BlockSpec((count, rows, HEAD_DIM), lambda h: (0, 0, h + first))


def constant(shape):
    return pl.BlockSpec(shape, lambda h: (0, 0))


def attend(place, doc, new, old):
    blocks = len(new)
    span, width = blocks * QB, new[0].shape[-1]
    heads = width // HEAD_DIM
    bf = jnp.bfloat16
    return pl.pallas_call(
        attend_kernel,
        grid=(heads,),
        in_specs=[pl.BlockSpec(memory_space=pltpu.SMEM), constant((1, span))]
        + [spec3(3, QB)] * blocks
        + [spec3(2, QB)] * blocks,
        out_specs=[spec2(span), constant((heads, span))],
        out_shape=[
            jax.ShapeDtypeStruct((span, width), bf),
            jax.ShapeDtypeStruct((heads, span), jnp.float32),
        ],
        scratch_shapes=[
            pltpu.VMEM((span, HEAD_DIM), bf),
            pltpu.VMEM((WINDOW + span, HEAD_DIM), bf),
            pltpu.VMEM((HEAD_DIM, WINDOW + span), bf),
        ],
        compiler_params=pltpu.CompilerParams(vmem_limit_bytes=ATTEND_LIMIT),
        cost_estimate=SMALL,
    )(place, doc, *new, *old)


def attend_back(place, doc, lse, new, old, cot, first, heads, kept=()):
    blocks = len(new)
    span, width = blocks * QB, new[0].shape[-1]
    bf, f32 = jnp.bfloat16, jnp.float32
    fixed = 3 + 3 * blocks
    return pl.pallas_call(
        functools.partial(back_kernel, first),
        grid=(heads,),
        in_specs=[
            pl.BlockSpec(memory_space=pltpu.SMEM),
            constant((1, span)),
            constant(lse.shape),
        ]
        + [spec3(3, QB, first)] * blocks
        + [spec3(2, QB, first)] * blocks
        + [spec2(QB, first)] * blocks
        + [pl.BlockSpec(memory_space=pl.ANY)] * len(kept),
        out_specs=[spec2(span, first)] * 3 + [spec3(2, WINDOW)],
        out_shape=[
            jax.ShapeDtypeStruct((span, width), bf),
            jax.ShapeDtypeStruct((span, width), f32),
            jax.ShapeDtypeStruct((span, width), f32),
            jax.ShapeDtypeStruct((2, WINDOW, heads * HEAD_DIM), bf),
        ],
        input_output_aliases={fixed + i: i for i in range(len(kept))},
        scratch_shapes=[pltpu.VMEM((span, HEAD_DIM), bf)] * 2
        + [pltpu.VMEM((WINDOW + span, HEAD_DIM), bf)] * 2
        + [pltpu.VMEM((HEAD_DIM, WINDOW + span), bf)]
        + [pltpu.VMEM((WINDOW + span, HEAD_DIM), f32)] * 2,
        compiler_params=pltpu.CompilerParams(vmem_limit_bytes=ATTEND_LIMIT),
        cost_estimate=SMALL,
    )(place, doc, lse, *new, *old, *cot, *kept)


PAIRS = [(0, 1), (1, 0), (2, 3), (3, 2)]
MIDDLE = [(1, 2), (2, 1)]
OUTWARD = [(1, 0), (2, 3)]
INWARD = [(0, 1), (3, 2)]


def send(block, route, axis="tp"):
    return lax.ppermute(block, axis, route)


def tie(*values):
    return lax.optimization_barrier(values)


def after(value, *others):
    return lax.optimization_barrier((value,) + others)[0]


def flip(bit, axis="fsdp"):
    return [(i, i ^ bit) for i in range(lax.axis_size(axis))]


def neighbour_route(distance, per_seq):
    size = lax.axis_size("fsdp")
    pairs = [(i - 1, i) for i in range(1, size) if i % per_seq]
    return pairs if distance > 0 else [(b, a) for a, b in pairs]


def pick(array, index, axis):
    return lax.dynamic_index_in_dim(array, index, axis, keepdims=False)


NORM_ROWS = 64


def row_mean(values):
    return jnp.mean(values, axis=-1, keepdims=True)


def total_of(first, *more):
    total = first.astype(jnp.float32)
    for array in more:
        total = total + array.astype(jnp.float32)
    return total


def norm_kernel(parts, gain_ref, *refs):
    total = total_of(*[ref[...] for ref in refs[:parts]])
    inverse = lax.rsqrt(row_mean(total * total) + EPS)
    refs[parts][...] = (total * inverse * gain_ref[...]).astype(jnp.bfloat16)
    refs[parts + 1][...] = jnp.broadcast_to(inverse, refs[parts + 1].shape)
    if len(refs) > parts + 2:
        refs[parts + 2][...] = total


def row_call(kernel, gain, arrays, outs, sums=0):
    rows, width = arrays[0].shape
    block = lambda w: pl.BlockSpec((NORM_ROWS, w), lambda r: (r, 0))
    one = pl.BlockSpec((1, width), lambda r: (0, 0))
    return pl.pallas_call(
        kernel,
        grid=(rows // NORM_ROWS,),
        in_specs=[one] + [block(a.shape[1]) for a in arrays],
        out_specs=[block(w) for w, _ in outs] + [one] * sums,
        out_shape=[jax.ShapeDtypeStruct((rows, w), t) for w, t in outs]
        + [jax.ShapeDtypeStruct((1, width), jnp.float32)] * sums,
        compiler_params=pltpu.CompilerParams(vmem_limit_bytes=VMEM_LIMIT),
        cost_estimate=SMALL,
    )(gain[None], *arrays)


def norm(gain, parts, keep):
    width = parts[0].shape[1]
    outs = [(width, jnp.bfloat16), (128, jnp.float32)] + [(width, jnp.float32)] * keep
    return row_call(functools.partial(norm_kernel, len(parts)), gain, parts, outs)


def norm_back_kernel(parts, gain_ref, *refs):
    grad = total_of(*[ref[...] for ref in refs[:parts]])
    value_ref, inverse_ref, more_ref = refs[parts : parts + 3]
    outs = refs[parts + 3 :]
    inverse = inverse_ref[:, :1]
    unit = value_ref[...].astype(jnp.float32) * inverse
    scaled = grad * gain_ref[...]
    result = more_ref[...].astype(jnp.float32) + inverse * (
        scaled - unit * row_mean(scaled * unit)
    )
    outs[0][...] = result.astype(jnp.bfloat16)
    if len(outs) == 3:
        outs[1][...] = result

        @pl.when(pl.program_id(0) == 0)
        def _():
            outs[2][...] = jnp.zeros_like(outs[2])

        outs[2][...] += jnp.sum(grad * unit, axis=0, keepdims=True)


def norm_back(gain, parts, value, inverse, more, keep):
    width = value.shape[1]
    outs = [(width, jnp.bfloat16)] + [(width, jnp.float32)] * keep
    return row_call(
        functools.partial(norm_back_kernel, len(parts)),
        gain,
        [*parts, value, inverse, more],
        outs,
        sums=int(keep),
    )


def add(a, b):
    return (a.astype(jnp.float32) + b.astype(jnp.float32)).astype(jnp.bfloat16)


def grad_kernel(blocks, which_ref, *refs):
    lhs, rhs = refs[:blocks], refs[blocks : 2 * blocks]
    away_ref, kept_ref, lhs_s, rhs_s = refs[2 * blocks :]
    count, e = away_ref.shape[1:3]
    group, groups = pl.program_id(0), pl.num_programs(0) // 2

    @pl.when(group == 0)
    def _():
        for k in range(blocks):
            for s in range(count):
                rhs_s[s * e : (s + 1) * e, k * QB : (k + 1) * QB] = rhs[k][s].T

    for k in range(blocks):
        lhs_s[k * QB : (k + 1) * QB] = lhs[k][...]

    def product(out_ref):
        for s in range(count):
            out_ref[0, s] = nn(rhs_s[s * e : (s + 1) * e], lhs_s[...]).astype(out_ref.dtype)

    pl.when(group < groups)(lambda: product(away_ref))
    pl.when(group >= groups)(lambda: product(kept_ref))


def grad_product(own, lhs, rhs):
    blocks = len(lhs)
    e = rhs[0][0].shape[-1]
    count = rhs[0][1]
    groups = lhs[0].shape[1] // (2 * QB)

    def lhs_at(j, own):
        parity = jnp.where(j < groups, 1 - own[0], own[0])
        return (0, 2 * lax.rem(j, groups) + parity)

    def rhs_at(array, k):
        at = (0, k, 0) if array.shape[0] == count else (k, 0, 0)
        return pl.BlockSpec((count, QB, e), lambda j, own: at)

    out = jax.ShapeDtypeStruct((groups, count, e, QB), jnp.bfloat16)
    return pl.pallas_call(
        functools.partial(grad_kernel, blocks),
        grid_spec=pltpu.PrefetchScalarGridSpec(
            num_scalar_prefetch=1,
            grid=(2 * groups,),
            in_specs=[pl.BlockSpec((QB, QB), lhs_at)] * blocks
            + [rhs_at(array, k) for array, _, k in rhs],
            out_specs=[
                pl.BlockSpec(
                    (1, count, e, QB), lambda j, own: (jnp.minimum(j, groups - 1), 0, 0, 0)
                ),
                pl.BlockSpec((1, count, e, QB), lambda j, own: (jnp.maximum(j - groups, 0), 0, 0, 0)),
            ],
            scratch_shapes=[
                pltpu.VMEM((blocks * QB, QB), jnp.bfloat16),
                pltpu.VMEM((count * e, blocks * QB), jnp.bfloat16),
            ],
        ),
        out_shape=[out, out],
        compiler_params=pltpu.CompilerParams(vmem_limit_bytes=VMEM_LIMIT),
        cost_estimate=SMALL,
    )(own.reshape(1).astype(jnp.int32), *lhs, *[r[0] for r in rhs])


def turn_kernel(group_ref, kept_ref, back_ref, *refs):
    total = kept_ref[0, 0].astype(jnp.float32) + back_ref[0, 0].astype(jnp.float32)
    for ref in refs[:-1]:
        total = total + ref[0].astype(jnp.float32)
    refs[-1][0] = total.T


def turn(group, kept, back, parts):
    groups, count, e, width = kept.shape
    mine = pl.BlockSpec((1, 1, e, width), lambda s, group: (group[0], s, 0, 0))
    return pl.pallas_call(
        turn_kernel,
        grid_spec=pltpu.PrefetchScalarGridSpec(
            num_scalar_prefetch=1,
            grid=(count,),
            in_specs=[mine, mine]
            + [pl.BlockSpec((1, e, width), lambda s, group: (s, 0, 0))] * len(parts),
            out_specs=pl.BlockSpec((1, width, e), lambda s, group: (s, 0, 0)),
        ),
        out_shape=jax.ShapeDtypeStruct((count, width, e), jnp.float32),
        compiler_params=pltpu.CompilerParams(vmem_limit_bytes=VMEM_LIMIT),
        cost_estimate=SMALL,
    )(group.reshape(1).astype(jnp.int32), kept, back, *parts)


def rows_kernel(blocks, *refs):
    w_ref, out_ref = refs[blocks], refs[blocks + 1]
    for k in range(blocks):
        out_ref[k * QB : (k + 1) * QB] = nn(refs[k][...], w_ref[...]).astype(out_ref.dtype)


def rows_product(lhs, w):
    blocks, inner, cols = len(lhs), w.shape[0], w.shape[1]
    wide = 512
    return pl.pallas_call(
        functools.partial(rows_kernel, blocks),
        grid=(cols // wide,),
        in_specs=[pl.BlockSpec((QB, inner), lambda n: (0, 0))] * blocks
        + [pl.BlockSpec((inner, wide), lambda n: (0, n))],
        out_specs=pl.BlockSpec((blocks * QB, wide), lambda n: (0, n)),
        out_shape=jax.ShapeDtypeStruct((blocks * QB, cols), jnp.bfloat16),
        compiler_params=pltpu.CompilerParams(vmem_limit_bytes=VMEM_LIMIT),
        cost_estimate=SMALL,
    )(*lhs, w)


class GradSum:
    def __init__(self, lhs, rhs, direct):
        me = lax.axis_index("fsdp")
        self.low, self.one, self.two = me % 2, (me // 2) % 2, me // 4
        self.group = me // 2
        self.lhs, self.rhs, self.direct = lhs, rhs, direct
        self.staged = lax.axis_size("fsdp") == 8
        self.back, self.parts = jnp.zeros((), jnp.bfloat16), []

    def product(self, *others):
        own = self.low if self.staged else jnp.int32(1)
        self.away, self.kept = grad_product(after(own, *others), self.lhs, self.rhs)

    def swap(self):
        if self.staged:
            self.back = send(self.away, flip(1), "fsdp")

    def half(self, index, axis, top, *more):
        groups, s, e, width = self.kept.shape
        start, size = [0] * 5, [2, 2, s, e // 2, width]
        start[axis], size[axis] = index, 1
        start[3] = 0 if top else e // 2
        cuts = [
            jnp.squeeze(lax.dynamic_slice(a.reshape(2, 2, s, e, width), start, size), axis)
            for a in (self.kept, self.back)
        ]
        return total_of(*cuts, *more).astype(jnp.bfloat16)

    def split(self):
        if self.staged and self.direct:
            self.parts = [
                total_of(pick(self.kept, self.group ^ k, 0), pick(self.back, self.group ^ k, 0))
                for k in (1, 2, 3)
            ]
            self.parts = [part.astype(jnp.bfloat16) for part in self.parts]
        elif self.staged:
            self.parts = [self.half(1 - self.one, 1, True), self.half(1 - self.two, 0, False)]

    def spread(self):
        routes = (2, 4, 6) if self.direct else (2, 4)
        self.parts = [send(p, flip(r), "fsdp") for p, r in zip(self.parts, routes)]

    def refine(self):
        if self.staged:
            self.a = self.half(self.one, 1, True, self.parts[0])
            self.b = self.half(self.two, 0, False, self.parts[1])
            self.parts = [pick(self.a, 1 - self.two, 0), pick(self.b, 1 - self.one, 0)]

    def finish(self):
        self.parts = [send(p, flip(r), "fsdp") for p, r in zip(self.parts, (4, 2))]

    def own(self, turned, *others):
        if not self.staged:
            both = jnp.stack([self.away, self.kept], axis=1)
            groups, _, s, e, width = both.shape
            both = both.transpose(2, 3, 0, 1, 4).reshape(s, e, 2 * groups * width)
            own = lax.psum_scatter(both, "fsdp", scatter_dimension=2, tiled=True)
            own = own.astype(jnp.float32)
            return own.transpose(0, 2, 1) if turned else own
        parts = tie(*self.parts, *others)[: len(self.parts)]
        if not self.direct:
            top = total_of(pick(self.a, self.two, 0), parts[0])
            bottom = total_of(pick(self.b, self.one, 0), parts[1])
            own = jnp.concatenate([top, bottom], axis=1)
            return own.transpose(0, 2, 1) if turned else own
        if turned:
            return turn(self.group, self.kept, self.back, parts)
        return total_of(pick(self.kept, self.group, 0), pick(self.back, self.group, 0), *parts)


def join(sums, *values):
    held = [[s.away, s.kept, s.back, *s.parts] for s in sums]
    tied = list(tie(*values, *[h for hs in held for h in hs]))
    out, tied = tied[: len(values)], tied[len(values) :]
    for s, hs in zip(sums, held):
        s.away, s.kept, s.back, *s.parts = tied[: len(hs)]
        tied = tied[len(hs) :]
    return out


def per_device(layer_input, norm_gains, w_qkv, w_out, w_gate_up, w_down, doc_start, out_cotangent):
    bf, f32 = jnp.bfloat16, jnp.float32
    span_len = doc_start.shape[0]
    me = lax.axis_index("tp")
    mid = (me == 1) | (me == 2)
    per_seq = SEQ_LEN // span_len
    place = jnp.stack([lax.axis_index("fsdp") * span_len, me]).astype(jnp.int32)
    doc_row = doc_start.reshape(1, span_len)
    full_qkv = lax.all_gather(w_qkv, "fsdp", axis=1, tiled=True)
    full_out = lax.all_gather(w_out, "fsdp", axis=1, tiled=True)
    forth, back = neighbour_route(1, per_seq), neighbour_route(-1, per_seq)

    normed_one, inverse_one = norm(norm_gains[0], [layer_input], False)
    xm, x1 = send(normed_one, MIDDLE), send(normed_one, PAIRS)
    xo, xf = send(xm, OUTWARD), send(x1, MIDDLE)
    full_qkv = after(full_qkv, x1)

    def project(block):
        return jnp.einsum("td,sde->ste", block, full_qkv, preferred_element_type=f32).astype(bf)

    first = project(normed_one)
    xf, xo, first = tie(xf, xo, first)
    x2 = jnp.where(mid, xf, xo)
    x3 = send(xf, OUTWARD)
    attn_rows = [normed_one, x1, x2]
    new = [first, project(x1), project(x2)]
    old = [send(n[1:], forth, "fsdp") for n in new]
    x3, *old = tie(x3, *old)
    attn_rows.append(jnp.where(mid, xm, x3))
    new.append(project(attn_rows[3]))
    old.append(send(new[3][1:], forth, "fsdp"))
    old[3], w_gate_up, w_down = tie(old[3], w_gate_up, w_down)
    full_gate_up = lax.all_gather(w_gate_up, "fsdp", axis=1, tiled=True)
    full_down = lax.all_gather(w_down, "fsdp", axis=1, tiled=True)
    late_cot = after(out_cotangent, new[3])
    c1, cm = send(late_cot, PAIRS), send(late_cot, MIDDLE)
    heads_out, lse = attend(place, doc_row, new, old)

    def out_part(k):
        return nn(heads_out[k * QB : (k + 1) * QB], full_out).astype(bf)

    def cross(middle, end):
        return send(jnp.where(mid, middle, end), PAIRS)

    a3 = out_part(3)
    y1 = cross(after(cm, a3), a3)
    c1 = after(c1, a3)
    cf = send(c1, MIDDLE)
    a2, a1, a0 = out_part(2), out_part(1), out_part(0)
    y1, cf, a2, a1, a0 = tie(y1, cf, a2, a1, a0)
    y2, t3 = cross(cf, a2), send(add(a2, y1), MIDDLE)
    y2, t3 = tie(y2, t3)
    t4, t5 = send(add(a3, y2), MIDDLE), send(add(a1, t3), PAIRS)
    cot = [out_cotangent, c1, jnp.where(mid, cf, y1), jnp.where(mid, cm, y2)]
    t4, t5 = tie(t4, t5)
    normed_two, inverse_two, residual_mid = norm(norm_gains[1], [layer_input, a0, t4, t5], True)

    def up(rows):
        return jnp.einsum("td,sdf->stf", rows, full_gate_up, preferred_element_type=f32)

    def down(gate_up, cot_rows):
        gate_pre, up_pre = gate_up[0], gate_up[1]
        sig = jax.nn.sigmoid(gate_pre)
        act = (gate_pre * sig * up_pre).astype(bf)
        grad_act = nt(cot_rows, full_down)
        grad_up = grad_act * gate_pre * sig
        grad_gate = grad_act * up_pre * sig * (1.0 + gate_pre * (1.0 - sig))
        return act, jnp.stack([grad_gate, grad_up]).astype(bf)

    def second_back(grads):
        return jnp.einsum("stf,sdf->td", grads, full_gate_up, preferred_element_type=f32).astype(bf)

    m1, mm = send(normed_two, PAIRS), send(normed_two, MIDDLE)
    u0 = up(normed_two)
    m1, mm, u0 = tie(m1, mm, u0)
    mo, mf = send(mm, OUTWARD), send(m1, MIDDLE)
    u1 = up(m1)
    f0 = down(after(u0, u1), cot[0])
    mf, mo, u1, f0 = tie(mf, mo, u1, f0)
    m2 = jnp.where(mid, mf, mo)
    m3 = send(mf, OUTWARD)
    f1 = down(u1, cot[1])
    f2 = down(up(m2), cot[2])
    g0, g1, g2 = second_back(f0[1]), second_back(f1[1]), second_back(f2[1])
    m3, f1, f2, g0, g1, g2 = tie(m3, f1, f2, g0, g1, g2)
    m3 = jnp.where(mid, mm, m3)
    f3 = down(up(m3), cot[3])
    g3 = second_back(f3[1])

    feed = (f0, f1, f2, f3)
    t1 = send(g3, INWARD)
    up_sum = GradSum([normed_two, m1, m2, m3], [(f[1], 2, 0) for f in feed], False)
    up_sum.product(g3)
    (t1,) = join([up_sum], t1)
    t2, t3 = send(after(g2, t1), INWARD), send(add(g2, t1), MIDDLE)
    up_sum.swap()
    down_sum = GradSum(cot, [(f[0][None], 1, 0) for f in feed], False)
    down_sum.product(t1)
    t2, t3 = join([up_sum, down_sum], t2, t3)
    t4, t5 = send(add(g3, t2), MIDDLE), send(add(g1, t3), PAIRS)
    down_sum.swap()
    up_sum.split()
    down_part = rows_product([f[0] for f in feed[:3]] + [after(f3[0], t2)], full_down)
    t4, t5, down_part = join([up_sum, down_sum], t4, t5, down_part)
    grad_branch, grad_mid, gain_two = norm_back(
        norm_gains[1], [g0, t4, t5], residual_mid, inverse_two, out_cotangent, True
    )

    def heads_back(block):
        return nt(block, full_out).astype(bf)

    d3, d2, d1, d0 = [down_part[k * QB : (k + 1) * QB] for k in (3, 2, 1, 0)]
    b1, bm = send(grad_branch, PAIRS), send(grad_branch, MIDDLE)
    up_sum.spread()
    down_sum.kept = after(down_sum.kept, grad_branch)
    down_sum.split()
    h0 = heads_back(grad_branch)
    b1, bm, h0 = join([down_sum], b1, bm, h0)
    y1, bfar = cross(bm, d3), send(b1, MIDDLE)
    down_sum.spread()
    h1 = heads_back(b1)
    y1, bfar, h1 = join([up_sum], y1, bfar, h1)
    b2 = jnp.where(mid, bfar, y1)
    y2, r3 = cross(bfar, d2), send(add(d2, y1), MIDDLE)
    up_sum.refine()
    h2 = heads_back(b2)
    y2, r3, h2 = join([up_sum, down_sum], y2, r3, h2)
    b3 = jnp.where(mid, bm, y2)
    h3 = heads_back(b3)
    r4, r5 = send(add(d3, y2), MIDDLE), send(add(d1, r3), PAIRS)
    up_sum.finish()
    cots = [h0, h1, h2, h3]
    half = heads_out.shape[1] // HEAD_DIM // 2
    *kept, prev_a = attend_back(place, doc_row, lse, new, old, cots, 0, half)
    head_blocks = heads_out.reshape(4, QB, -1)
    gb_blocks = [grad_branch, b1, b2, b3]
    out_sum = GradSum(gb_blocks, [(head_blocks, 1, k) for k in range(4)], True)
    out_sum.product(h3)
    r4, r5, prev_a, *kept = join([out_sum, up_sum, down_sum], r4, r5, prev_a, *kept)
    n_a = send(prev_a, back, "fsdp")
    out_sum.swap()
    *kept, prev_b = attend_back(place, doc_row, lse, new, old, cots, half, half, kept)
    n_a, prev_b, *kept = join([out_sum, down_sum], n_a, prev_b, *kept)
    n_b = send(prev_b, back, "fsdp")
    grad_q, own_k, own_v = kept
    out_sum.split()
    down_sum.refine()
    (n_b,) = join([out_sum, down_sum], n_b)

    def piece(rows):
        arrived = jnp.concatenate([n_a[:, rows], n_b[:, rows]], axis=2)
        return jnp.stack([grad_q[rows], add(own_k[rows], arrived[0]), add(own_v[rows], arrived[1])])

    def first_back(grad):
        return jnp.einsum("ste,sde->td", grad, full_qkv, preferred_element_type=f32).astype(bf)

    last = slice(3 * QB, 4 * QB)
    q3 = piece(last)
    p3 = first_back(q3)
    t1 = send(p3, INWARD)
    out_sum.parts = [after(p, p3) for p in out_sum.parts]
    down_sum.parts = [after(p, p3) for p in down_sum.parts]
    out_sum.spread()
    down_sum.finish()
    q012 = after(piece(slice(0, 3 * QB)), p3)
    p012 = first_back(q012)
    qkv_sum = GradSum(attn_rows, [(q012, 3, k) for k in range(3)] + [(q3, 3, 0)], True)
    qkv_sum.product(p3)
    t1, p012, p3 = join([qkv_sum, out_sum, down_sum], t1, p012, p3)
    p0, p1, p2 = [p012[k * QB : (k + 1) * QB] for k in range(3)]
    t2, t3 = send(p2, INWARD), send(add(p2, t1), MIDDLE)
    qkv_sum.swap()
    qkv_sum.split()
    qkv_sum.spread()
    late = tie(p0, p1, p2, p3, qkv_sum.back)[:4]
    gain_one = functools.reduce(
        jnp.add,
        [jnp.sum(p.astype(f32) * r.astype(f32), axis=0) for p, r in zip(late, attn_rows)],
    )
    gains = jnp.stack([gain_one / norm_gains[0], gain_two[0]])
    if lax.axis_size("fsdp") == 8:
        gains = [gains] + [send(gains, flip(k), "fsdp") for k in range(1, 8)]
    else:
        gains = [lax.psum(gains, "fsdp")]
    down_own = down_sum.own(False)
    up_own = up_sum.own(True, qkv_sum.back)
    t2, t3, down_own, up_own, *gains = tie(t2, t3, down_own, up_own, *gains)
    t4, t5 = send(add(p3, t2), MIDDLE), send(add(p1, t3), PAIRS)
    gains = total_of(*gains)
    out_own = out_sum.own(False, t2)
    layer_output = (
        residual_mid + (d0.astype(f32) + r4.astype(f32) + after(r5, t2).astype(f32))
    ).astype(bf)
    t4, t5, gains, layer_output, out_own = tie(t4, t5, gains, layer_output, out_own)
    gains = total_of(gains, *[send(gains, flip(k, "tp"), "tp") for k in (1, 2, 3)])
    (input_grad,) = norm_back(
        norm_gains[0], [p0, t4, t5], layer_input, inverse_one, grad_mid, False
    )
    qkv_own = qkv_sum.own(True, t5)
    return (layer_output, input_grad, gains, qkv_own, out_own[0], up_own, down_own[0])


def solution(mesh):
    in_specs = (
        P(("fsdp", "tp"), None),
        P(),
        P(None, "fsdp", "tp"),
        P("tp", "fsdp"),
        P(None, "fsdp", "tp"),
        P("tp", "fsdp"),
        P("fsdp"),
        P(("fsdp", "tp"), None),
    )
    out_specs = (
        P(("fsdp", "tp"), None),
        P(("fsdp", "tp"), None),
        P(),
        P(None, "fsdp", "tp"),
        P("tp", "fsdp"),
        P(None, "fsdp", "tp"),
        P("tp", "fsdp"),
    )
    return jax.shard_map(
        per_device, mesh=mesh, in_specs=in_specs, out_specs=out_specs, check_vma=False
    )
```

```python
import functools
import math

import jax
import jax.numpy as jnp
from jax import lax
from jax.experimental import pallas as pl
from jax.experimental.pallas import tpu as pltpu
from jax.sharding import PartitionSpec as P

HEAD_DIM = 128
WINDOW = 1024
SEQ_LEN = 4096
QB = 256
SCALE = 1.0 / math.sqrt(HEAD_DIM)
LOG2E = 1.4426950408889634
EPS = 1e-06
MASKED = -1e30
VMEM_LIMIT = 36 << 20
ATTEND_LIMIT = 60 << 20
SMALL = pl.CostEstimate(flops=1 << 20, bytes_accessed=1 << 16, transcendentals=0)
NT = (((1,), (1,)), ((), ()))
TN = (((0,), (0,)), ((), ()))


def nt(a, b):
    return lax.dot_general(a, b, NT, preferred_element_type=jnp.float32)


def nn(a, b):
    return jnp.dot(a, b, preferred_element_type=jnp.float32)


def tn(a, b):
    return lax.dot_general(a, b, TN, preferred_element_type=jnp.float32)


def masked_scores(k_j, q, j, lo):
    s = nt(k_j, q)
    row = lax.broadcasted_iota(jnp.int32, s.shape, 0) + j * QB
    ok = row >= lo
    if (j + 1) * QB > WINDOW:
        hi = lax.broadcasted_iota(jnp.int32, (1, QB), 1) + WINDOW
        ok = ok & (row <= hi)
    return jnp.where(ok, s, MASKED)


def low_bound(doc_ref, b, off):
    q_row = lax.broadcasted_iota(jnp.int32, (1, QB), 1)
    doc = doc_ref[:, b * QB : (b + 1) * QB]
    return jnp.maximum(q_row + 1, doc - off + (WINDOW - b * QB))


def block_at(index):
    return pl.ds(pl.multiple_of(index * QB, QB), QB)


def attend_kernel(place_ref, doc_ref, *refs):
    new, old = refs[:4], refs[4:8]
    o_ref, lse_ref, q_s, k_s, vt_s = refs[8:]
    h = pl.program_id(0)
    off, me = place_ref[0], place_ref[1]
    blocks = len(new)
    for slot in range(blocks):
        at = me ^ slot
        q_s[block_at(at)] = new[slot][0]
        k_s[block_at(at)] = old[slot][0]
        k_s[block_at(at + blocks)] = new[slot][1]
        vt_s[:, block_at(at)] = old[slot][1].T
        vt_s[:, block_at(at + blocks)] = new[slot][2].T
    c = SCALE * LOG2E
    n = WINDOW // QB + 1
    for b in range(blocks):
        q = q_s[b * QB : (b + 1) * QB]
        lo = low_bound(doc_ref, b, off)
        ss = [
            masked_scores(k_s[(b + j) * QB : (b + j + 1) * QB], q, j, lo) for j in range(n)
        ]
        m = functools.reduce(jnp.maximum, [jnp.max(s, axis=0, keepdims=True) for s in ss])
        total = jnp.zeros((1, QB), jnp.float32)
        acc = jnp.zeros((HEAD_DIM, QB), jnp.float32)
        for j in range(n):
            p = jnp.exp2((ss[j] - m) * c)
            total = total + jnp.sum(p, axis=0, keepdims=True)
            acc = acc + nn(vt_s[:, (b + j) * QB : (b + j + 1) * QB], p.astype(jnp.bfloat16))
        o_ref[block_at(me ^ b)] = (acc / total).T.astype(o_ref.dtype)
        lse_ref[pl.ds(h, 1), b * QB : (b + 1) * QB] = m * c + jnp.log2(total)


def back_kernel(first, place_ref, doc_ref, lse_ref, *refs):
    new, old, cot = refs[:4], refs[4:8], refs[8:12]
    dq_ref, dk_ref, dv_ref, prev_ref, q_s, do_s, k_s, v_s, kt_s, dk_s, dv_s = refs[-11:]
    h = pl.program_id(0)
    off, me = place_ref[0], place_ref[1]
    blocks = len(new)
    for slot in range(blocks):
        at = me ^ slot
        q_s[block_at(at)] = new[slot][0]
        do_s[block_at(at)] = cot[slot][...]
        k_s[block_at(at)] = old[slot][0]
        k_s[block_at(at + blocks)] = new[slot][1]
        v_s[block_at(at)] = old[slot][1]
        v_s[block_at(at + blocks)] = new[slot][2]
        kt_s[:, block_at(at)] = old[slot][0].T
        kt_s[:, block_at(at + blocks)] = new[slot][1].T
    c = SCALE * LOG2E
    n = WINDOW // QB + 1
    seen = 0
    for b in range(blocks):
        q = q_s[b * QB : (b + 1) * QB]
        do = do_s[b * QB : (b + 1) * QB]
        lse = lse_ref[pl.ds(h + first, 1), b * QB : (b + 1) * QB]
        lo = low_bound(doc_ref, b, off)
        delta = jnp.zeros((1, QB), jnp.float32)
        ps, dps = [], []
        for j in range(n):
            rows = slice((b + j) * QB, (b + j + 1) * QB)
            p = jnp.exp2(masked_scores(k_s[rows], q, j, lo) * c - lse)
            dp = nt(v_s[rows], do)
            delta = delta + jnp.sum(p * dp, axis=0, keepdims=True)
            dv = nn(p.astype(jnp.bfloat16), do)
            if b + j >= seen:
                dv_s[rows] = dv
            else:
                dv_s[rows] += dv
            ps.append(p)
            dps.append(dp)
        dqt = jnp.zeros((HEAD_DIM, QB), jnp.float32)
        for j in range(n):
            rows = slice((b + j) * QB, (b + j + 1) * QB)
            ds = (ps[j] * (dps[j] - delta)).astype(jnp.bfloat16)
            dk = nn(ds, q)
            if b + j >= seen:
                dk_s[rows] = dk
            else:
                dk_s[rows] += dk
            dqt = dqt + nn(kt_s[:, rows], ds)
        seen = b + n
        dq_ref[block_at(me ^ b)] = (dqt * SCALE).T.astype(dq_ref.dtype)
    for slot in range(blocks):
        at = me ^ slot
        rows = slice(slot * QB, (slot + 1) * QB)
        prev_ref[0, rows] = (dk_s[block_at(at)] * SCALE).astype(prev_ref.dtype)
        prev_ref[1, rows] = dv_s[block_at(at)].astype(prev_ref.dtype)
        dk_ref[rows] = dk_s[block_at(at + blocks)] * SCALE
        dv_ref[rows] = dv_s[block_at(at + blocks)]


def spec2(rows, first=0):
    return pl.BlockSpec((rows, HEAD_DIM), lambda h: (0, h + first))


def spec3(count, rows, first=0):
    return pl.BlockSpec((count, rows, HEAD_DIM), lambda h: (0, 0, h + first))


def constant(shape):
    return pl.BlockSpec(shape, lambda h: (0, 0))


def attend(place, doc, new, old):
    blocks = len(new)
    span, width = blocks * QB, new[0].shape[-1]
    heads = width // HEAD_DIM
    bf = jnp.bfloat16
    return pl.pallas_call(
        attend_kernel,
        grid=(heads,),
        in_specs=[pl.BlockSpec(memory_space=pltpu.SMEM), constant((1, span))]
        + [spec3(3, QB)] * blocks
        + [spec3(2, QB)] * blocks,
        out_specs=[spec2(span), constant((heads, span))],
        out_shape=[
            jax.ShapeDtypeStruct((span, width), bf),
            jax.ShapeDtypeStruct((heads, span), jnp.float32),
        ],
        scratch_shapes=[
            pltpu.VMEM((span, HEAD_DIM), bf),
            pltpu.VMEM((WINDOW + span, HEAD_DIM), bf),
            pltpu.VMEM((HEAD_DIM, WINDOW + span), bf),
        ],
        compiler_params=pltpu.CompilerParams(vmem_limit_bytes=ATTEND_LIMIT),
        cost_estimate=SMALL,
    )(place, doc, *new, *old)


def attend_back(place, doc, lse, new, old, cot, first, heads, kept=()):
    blocks = len(new)
    span, width = blocks * QB, new[0].shape[-1]
    bf, f32 = jnp.bfloat16, jnp.float32
    fixed = 3 + 3 * blocks
    return pl.pallas_call(
        functools.partial(back_kernel, first),
        grid=(heads,),
        in_specs=[
            pl.BlockSpec(memory_space=pltpu.SMEM),
            constant((1, span)),
            constant(lse.shape),
        ]
        + [spec3(3, QB, first)] * blocks
        + [spec3(2, QB, first)] * blocks
        + [spec2(QB, first)] * blocks
        + [pl.BlockSpec(memory_space=pl.ANY)] * len(kept),
        out_specs=[spec2(span, first)] * 3 + [spec3(2, WINDOW)],
        out_shape=[
            jax.ShapeDtypeStruct((span, width), bf),
            jax.ShapeDtypeStruct((span, width), f32),
            jax.ShapeDtypeStruct((span, width), f32),
            jax.ShapeDtypeStruct((2, WINDOW, heads * HEAD_DIM), bf),
        ],
        input_output_aliases={fixed + i: i for i in range(len(kept))},
        scratch_shapes=[pltpu.VMEM((span, HEAD_DIM), bf)] * 2
        + [pltpu.VMEM((WINDOW + span, HEAD_DIM), bf)] * 2
        + [pltpu.VMEM((HEAD_DIM, WINDOW + span), bf)]
        + [pltpu.VMEM((WINDOW + span, HEAD_DIM), f32)] * 2,
        compiler_params=pltpu.CompilerParams(vmem_limit_bytes=ATTEND_LIMIT),
        cost_estimate=SMALL,
    )(place, doc, lse, *new, *old, *cot, *kept)


PAIRS = [(0, 1), (1, 0), (2, 3), (3, 2)]
MIDDLE = [(1, 2), (2, 1)]
OUTWARD = [(1, 0), (2, 3)]
INWARD = [(0, 1), (3, 2)]


def send(block, route, axis="tp"):
    return lax.ppermute(block, axis, route)


def tie(*values):
    return lax.optimization_barrier(values)


def after(value, *others):
    return lax.optimization_barrier((value,) + others)[0]


def flip(bit, axis="fsdp"):
    return [(i, i ^ bit) for i in range(lax.axis_size(axis))]


def neighbour_route(distance, per_seq):
    size = lax.axis_size("fsdp")
    pairs = [(i - 1, i) for i in range(1, size) if i % per_seq]
    return pairs if distance > 0 else [(b, a) for a, b in pairs]


def pick(array, index, axis):
    return lax.dynamic_index_in_dim(array, index, axis, keepdims=False)


NORM_ROWS = 64


def row_mean(values):
    return jnp.mean(values, axis=-1, keepdims=True)


def total_of(first, *more):
    total = first.astype(jnp.float32)
    for array in more:
        total = total + array.astype(jnp.float32)
    return total


def norm_kernel(parts, gain_ref, *refs):
    total = total_of(*[ref[...] for ref in refs[:parts]])
    inverse = lax.rsqrt(row_mean(total * total) + EPS)
    refs[parts][...] = (total * inverse * gain_ref[...]).astype(jnp.bfloat16)
    refs[parts + 1][...] = jnp.broadcast_to(inverse, refs[parts + 1].shape)
    if len(refs) > parts + 2:
        refs[parts + 2][...] = total


def row_call(kernel, gain, arrays, outs, sums=0):
    rows, width = arrays[0].shape
    block = lambda w: pl.BlockSpec((NORM_ROWS, w), lambda r: (r, 0))
    one = pl.BlockSpec((1, width), lambda r: (0, 0))
    return pl.pallas_call(
        kernel,
        grid=(rows // NORM_ROWS,),
        in_specs=[one] + [block(a.shape[1]) for a in arrays],
        out_specs=[block(w) for w, _ in outs] + [one] * sums,
        out_shape=[jax.ShapeDtypeStruct((rows, w), t) for w, t in outs]
        + [jax.ShapeDtypeStruct((1, width), jnp.float32)] * sums,
        compiler_params=pltpu.CompilerParams(vmem_limit_bytes=VMEM_LIMIT),
        cost_estimate=SMALL,
    )(gain[None], *arrays)


def norm(gain, parts, keep):
    width = parts[0].shape[1]
    outs = [(width, jnp.bfloat16), (128, jnp.float32)] + [(width, jnp.float32)] * keep
    return row_call(functools.partial(norm_kernel, len(parts)), gain, parts, outs)


def norm_back_kernel(parts, gain_ref, *refs):
    grad = total_of(*[ref[...] for ref in refs[:parts]])
    value_ref, inverse_ref, more_ref = refs[parts : parts + 3]
    outs = refs[parts + 3 :]
    inverse = inverse_ref[:, :1]
    unit = value_ref[...].astype(jnp.float32) * inverse
    scaled = grad * gain_ref[...]
    result = more_ref[...].astype(jnp.float32) + inverse * (
        scaled - unit * row_mean(scaled * unit)
    )
    outs[0][...] = result.astype(jnp.bfloat16)
    if len(outs) == 3:
        outs[1][...] = result

        @pl.when(pl.program_id(0) == 0)
        def _():
            outs[2][...] = jnp.zeros_like(outs[2])

        outs[2][...] += jnp.sum(grad * unit, axis=0, keepdims=True)


def norm_back(gain, parts, value, inverse, more, keep):
    width = value.shape[1]
    outs = [(width, jnp.bfloat16)] + [(width, jnp.float32)] * keep
    return row_call(
        functools.partial(norm_back_kernel, len(parts)),
        gain,
        [*parts, value, inverse, more],
        outs,
        sums=int(keep),
    )


def add(a, b):
    return (a.astype(jnp.float32) + b.astype(jnp.float32)).astype(jnp.bfloat16)


def grad_kernel(blocks, which_ref, *refs):
    lhs, rhs = refs[:blocks], refs[blocks : 2 * blocks]
    away_ref, kept_ref, lhs_s, rhs_s = refs[2 * blocks :]
    count, e = away_ref.shape[1:3]
    group, groups = pl.program_id(0), pl.num_programs(0) // 2

    @pl.when(group == 0)
    def _():
        for k in range(blocks):
            for s in range(count):
                rhs_s[s * e : (s + 1) * e, k * QB : (k + 1) * QB] = rhs[k][s].T

    for k in range(blocks):
        lhs_s[k * QB : (k + 1) * QB] = lhs[k][...]

    def product(out_ref):
        for s in range(count):
            out_ref[0, s] = nn(rhs_s[s * e : (s + 1) * e], lhs_s[...]).astype(out_ref.dtype)

    pl.when(group < groups)(lambda: product(away_ref))
    pl.when(group >= groups)(lambda: product(kept_ref))


def grad_product(own, lhs, rhs):
    blocks = len(lhs)
    e = rhs[0][0].shape[-1]
    count = rhs[0][1]
    groups = lhs[0].shape[1] // (2 * QB)

    def lhs_at(j, own):
        parity = jnp.where(j < groups, 1 - own[0], own[0])
        return (0, 2 * lax.rem(j, groups) + parity)

    def rhs_at(array, k):
        at = (0, k, 0) if array.shape[0] == count else (k, 0, 0)
        return pl.BlockSpec((count, QB, e), lambda j, own: at)

    out = jax.ShapeDtypeStruct((groups, count, e, QB), jnp.bfloat16)
    return pl.pallas_call(
        functools.partial(grad_kernel, blocks),
        grid_spec=pltpu.PrefetchScalarGridSpec(
            num_scalar_prefetch=1,
            grid=(2 * groups,),
            in_specs=[pl.BlockSpec((QB, QB), lhs_at)] * blocks
            + [rhs_at(array, k) for array, _, k in rhs],
            out_specs=[
                pl.BlockSpec(
                    (1, count, e, QB), lambda j, own: (jnp.minimum(j, groups - 1), 0, 0, 0)
                ),
                pl.BlockSpec((1, count, e, QB), lambda j, own: (jnp.maximum(j - groups, 0), 0, 0, 0)),
            ],
            scratch_shapes=[
                pltpu.VMEM((blocks * QB, QB), jnp.bfloat16),
                pltpu.VMEM((count * e, blocks * QB), jnp.bfloat16),
            ],
        ),
        out_shape=[out, out],
        compiler_params=pltpu.CompilerParams(vmem_limit_bytes=VMEM_LIMIT),
        cost_estimate=SMALL,
    )(own.reshape(1).astype(jnp.int32), *lhs, *[r[0] for r in rhs])


def turn_kernel(group_ref, kept_ref, back_ref, *refs):
    total = kept_ref[0, 0].astype(jnp.float32) + back_ref[0, 0].astype(jnp.float32)
    for ref in refs[:-1]:
        total = total + ref[0].astype(jnp.float32)
    refs[-1][0] = total.T


def turn(group, kept, back, parts):
    groups, count, e, width = kept.shape
    mine = pl.BlockSpec((1, 1, e, width), lambda s, group: (group[0], s, 0, 0))
    return pl.pallas_call(
        turn_kernel,
        grid_spec=pltpu.PrefetchScalarGridSpec(
            num_scalar_prefetch=1,
            grid=(count,),
            in_specs=[mine, mine]
            + [pl.BlockSpec((1, e, width), lambda s, group: (s, 0, 0))] * len(parts),
            out_specs=pl.BlockSpec((1, width, e), lambda s, group: (s, 0, 0)),
        ),
        out_shape=jax.ShapeDtypeStruct((count, width, e), jnp.float32),
        compiler_params=pltpu.CompilerParams(vmem_limit_bytes=VMEM_LIMIT),
        cost_estimate=SMALL,
    )(group.reshape(1).astype(jnp.int32), kept, back, *parts)


def rows_kernel(blocks, *refs):
    w_ref, out_ref = refs[blocks], refs[blocks + 1]
    for k in range(blocks):
        out_ref[k * QB : (k + 1) * QB] = nn(refs[k][...], w_ref[...]).astype(out_ref.dtype)


def rows_product(lhs, w):
    blocks, inner, cols = len(lhs), w.shape[0], w.shape[1]
    wide = 512
    return pl.pallas_call(
        functools.partial(rows_kernel, blocks),
        grid=(cols // wide,),
        in_specs=[pl.BlockSpec((QB, inner), lambda n: (0, 0))] * blocks
        + [pl.BlockSpec((inner, wide), lambda n: (0, n))],
        out_specs=pl.BlockSpec((blocks * QB, wide), lambda n: (0, n)),
        out_shape=jax.ShapeDtypeStruct((blocks * QB, cols), jnp.bfloat16),
        compiler_params=pltpu.CompilerParams(vmem_limit_bytes=VMEM_LIMIT),
        cost_estimate=SMALL,
    )(*lhs, w)


class GradSum:
    def __init__(self, lhs, rhs, direct):
        me = lax.axis_index("fsdp")
        self.low, self.one, self.two = me % 2, (me // 2) % 2, me // 4
        self.group = me // 2
        self.lhs, self.rhs, self.direct = lhs, rhs, direct
        self.staged = lax.axis_size("fsdp") == 8
        self.back, self.parts = jnp.zeros((), jnp.bfloat16), []

    def product(self, *others):
        own = self.low if self.staged else jnp.int32(1)
        self.away, self.kept = grad_product(after(own, *others), self.lhs, self.rhs)

    def swap(self):
        if self.staged:
            self.back = send(self.away, flip(1), "fsdp")

    def half(self, index, axis, top, *more):
        groups, s, e, width = self.kept.shape
        start, size = [0] * 5, [2, 2, s, e // 2, width]
        start[axis], size[axis] = index, 1
        start[3] = 0 if top else e // 2
        cuts = [
            jnp.squeeze(lax.dynamic_slice(a.reshape(2, 2, s, e, width), start, size), axis)
            for a in (self.kept, self.back)
        ]
        return total_of(*cuts, *more).astype(jnp.bfloat16)

    def split(self):
        if self.staged and self.direct:
            self.parts = [
                total_of(pick(self.kept, self.group ^ k, 0), pick(self.back, self.group ^ k, 0))
                for k in (1, 2, 3)
            ]
            self.parts = [part.astype(jnp.bfloat16) for part in self.parts]
        elif self.staged:
            self.parts = [self.half(1 - self.one, 1, True), self.half(1 - self.two, 0, False)]

    def spread(self):
        routes = (2, 4, 6) if self.direct else (2, 4)
        self.parts = [send(p, flip(r), "fsdp") for p, r in zip(self.parts, routes)]

    def refine(self):
        if self.staged:
            self.a = self.half(self.one, 1, True, self.parts[0])
            self.b = self.half(self.two, 0, False, self.parts[1])
            self.parts = [pick(self.a, 1 - self.two, 0), pick(self.b, 1 - self.one, 0)]

    def finish(self):
        self.parts = [send(p, flip(r), "fsdp") for p, r in zip(self.parts, (4, 2))]

    def own(self, turned, *others):
        if not self.staged:
            both = jnp.stack([self.away, self.kept], axis=1)
            groups, _, s, e, width = both.shape
            both = both.transpose(2, 3, 0, 1, 4).reshape(s, e, 2 * groups * width)
            own = lax.psum_scatter(both, "fsdp", scatter_dimension=2, tiled=True)
            own = own.astype(jnp.float32)
            return own.transpose(0, 2, 1) if turned else own
        parts = tie(*self.parts, *others)[: len(self.parts)]
        if not self.direct:
            top = total_of(pick(self.a, self.two, 0), parts[0])
            bottom = total_of(pick(self.b, self.one, 0), parts[1])
            own = jnp.concatenate([top, bottom], axis=1)
            return own.transpose(0, 2, 1) if turned else own
        if turned:
            return turn(self.group, self.kept, self.back, parts)
        return total_of(pick(self.kept, self.group, 0), pick(self.back, self.group, 0), *parts)


def join(sums, *values):
    held = [[s.away, s.kept, s.back, *s.parts] for s in sums]
    tied = list(tie(*values, *[h for hs in held for h in hs]))
    out, tied = tied[: len(values)], tied[len(values) :]
    for s, hs in zip(sums, held):
        s.away, s.kept, s.back, *s.parts = tied[: len(hs)]
        tied = tied[len(hs) :]
    return out


def per_device(layer_input, norm_gains, w_qkv, w_out, w_gate_up, w_down, doc_start, out_cotangent):
    bf, f32 = jnp.bfloat16, jnp.float32
    span_len = doc_start.shape[0]
    me = lax.axis_index("tp")
    mid = (me == 1) | (me == 2)
    per_seq = SEQ_LEN // span_len
    place = jnp.stack([lax.axis_index("fsdp") * span_len, me]).astype(jnp.int32)
    doc_row = doc_start.reshape(1, span_len)
    full_qkv = lax.all_gather(w_qkv, "fsdp", axis=1, tiled=True)
    full_out = lax.all_gather(w_out, "fsdp", axis=1, tiled=True)
    forth, back = neighbour_route(1, per_seq), neighbour_route(-1, per_seq)

    normed_one, inverse_one = norm(norm_gains[0], [layer_input], False)
    xm, x1 = send(normed_one, MIDDLE), send(normed_one, PAIRS)
    xo, xf = send(xm, OUTWARD), send(x1, MIDDLE)
    full_qkv = after(full_qkv, x1)

    def project(block):
        return jnp.einsum("td,sde->ste", block, full_qkv, preferred_element_type=f32).astype(bf)

    first = project(normed_one)
    xf, xo, first = tie(xf, xo, first)
    x2 = jnp.where(mid, xf, xo)
    x3 = send(xf, OUTWARD)
    attn_rows = [normed_one, x1, x2]
    new = [first, project(x1), project(x2)]
    old = [send(n[1:], forth, "fsdp") for n in new]
    x3, *old = tie(x3, *old)
    attn_rows.append(jnp.where(mid, xm, x3))
    new.append(project(attn_rows[3]))
    old.append(send(new[3][1:], forth, "fsdp"))
    old[3], w_gate_up, w_down = tie(old[3], w_gate_up, w_down)
    full_gate_up = lax.all_gather(w_gate_up, "fsdp", axis=1, tiled=True)
    full_down = lax.all_gather(w_down, "fsdp", axis=1, tiled=True)
    late_cot = after(out_cotangent, new[3])
    c1, cm = send(late_cot, PAIRS), send(late_cot, MIDDLE)
    heads_out, lse = attend(place, doc_row, new, old)

    def out_part(k):
        return nn(heads_out[k * QB : (k + 1) * QB], full_out).astype(bf)

    def cross(middle, end):
        return send(jnp.where(mid, middle, end), PAIRS)

    a3 = out_part(3)
    y1 = cross(after(cm, a3), a3)
    c1 = after(c1, a3)
    cf = send(c1, MIDDLE)
    a2, a1, a0 = out_part(2), out_part(1), out_part(0)
    y1, cf, a2, a1, a0 = tie(y1, cf, a2, a1, a0)
    y2, t3 = cross(cf, a2), send(add(a2, y1), MIDDLE)
    y2, t3 = tie(y2, t3)
    t4, t5 = send(add(a3, y2), MIDDLE), send(add(a1, t3), PAIRS)
    cot = [out_cotangent, c1, jnp.where(mid, cf, y1), jnp.where(mid, cm, y2)]
    t4, t5 = tie(t4, t5)
    normed_two, inverse_two, residual_mid = norm(norm_gains[1], [layer_input, a0, t4, t5], True)

    def up(rows):
        return jnp.einsum("td,sdf->stf", rows, full_gate_up, preferred_element_type=f32)

    def down(gate_up, cot_rows):
        gate_pre, up_pre = gate_up[0], gate_up[1]
        sig = jax.nn.sigmoid(gate_pre)
        act = (gate_pre * sig * up_pre).astype(bf)
        grad_act = nt(cot_rows, full_down)
        grad_up = grad_act * gate_pre * sig
        grad_gate = grad_act * up_pre * sig * (1.0 + gate_pre * (1.0 - sig))
        return act, jnp.stack([grad_gate, grad_up]).astype(bf)

    def second_back(grads):
        return jnp.einsum("stf,sdf->td", grads, full_gate_up, preferred_element_type=f32).astype(bf)

    m1, mm = send(normed_two, PAIRS), send(normed_two, MIDDLE)
    u0 = up(normed_two)
    m1, mm, u0 = tie(m1, mm, u0)
    mo, mf = send(mm, OUTWARD), send(m1, MIDDLE)
    u1 = up(m1)
    f0 = down(after(u0, u1), cot[0])
    mf, mo, u1, f0 = tie(mf, mo, u1, f0)
    m2 = jnp.where(mid, mf, mo)
    m3 = send(mf, OUTWARD)
    f1 = down(u1, cot[1])
    f2 = down(up(m2), cot[2])
    g0, g1, g2 = second_back(f0[1]), second_back(f1[1]), second_back(f2[1])
    m3, f1, f2, g0, g1, g2 = tie(m3, f1, f2, g0, g1, g2)
    m3 = jnp.where(mid, mm, m3)
    f3 = down(up(m3), cot[3])
    g3 = second_back(f3[1])

    feed = (f0, f1, f2, f3)
    t1 = send(g3, INWARD)
    up_sum = GradSum([normed_two, m1, m2, m3], [(f[1], 2, 0) for f in feed], False)
    up_sum.product(g3)
    (t1,) = join([up_sum], t1)
    t2, t3 = send(after(g2, t1), INWARD), send(add(g2, t1), MIDDLE)
    up_sum.swap()
    down_sum = GradSum(cot, [(f[0][None], 1, 0) for f in feed], False)
    down_sum.product(t1)
    t2, t3 = join([up_sum, down_sum], t2, t3)
    t4, t5 = send(add(g3, t2), MIDDLE), send(add(g1, t3), PAIRS)
    down_sum.swap()
    up_sum.split()
    down_part = rows_product([f[0] for f in feed[:3]] + [after(f3[0], t2)], full_down)
    t4, t5, down_part = join([up_sum, down_sum], t4, t5, down_part)
    grad_branch, grad_mid, gain_two = norm_back(
        norm_gains[1], [g0, t4, t5], residual_mid, inverse_two, out_cotangent, True
    )

    def heads_back(block):
        return nt(block, full_out).astype(bf)

    d3, d2, d1, d0 = [down_part[k * QB : (k + 1) * QB] for k in (3, 2, 1, 0)]
    b1, bm = send(grad_branch, PAIRS), send(grad_branch, MIDDLE)
    up_sum.spread()
    down_sum.kept = after(down_sum.kept, grad_branch)
    down_sum.split()
    h0 = heads_back(grad_branch)
    b1, bm, h0 = join([down_sum], b1, bm, h0)
    y1, bfar = cross(bm, d3), send(b1, MIDDLE)
    down_sum.spread()
    h1 = heads_back(b1)
    y1, bfar, h1 = join([up_sum], y1, bfar, h1)
    b2 = jnp.where(mid, bfar, y1)
    y2, r3 = cross(bfar, d2), send(add(d2, y1), MIDDLE)
    up_sum.refine()
    h2 = heads_back(b2)
    y2, r3, h2 = join([up_sum, down_sum], y2, r3, h2)
    b3 = jnp.where(mid, bm, y2)
    h3 = heads_back(b3)
    r4, r5 = send(add(d3, y2), MIDDLE), send(add(d1, r3), PAIRS)
    up_sum.finish()
    cots = [h0, h1, h2, h3]
    half = heads_out.shape[1] // HEAD_DIM // 2
    *kept, prev_a = attend_back(place, doc_row, lse, new, old, cots, 0, half)
    head_blocks = heads_out.reshape(4, QB, -1)
    gb_blocks = [grad_branch, b1, b2, b3]
    out_sum = GradSum(gb_blocks, [(head_blocks, 1, k) for k in range(4)], True)
    out_sum.product(h3)
    r4, r5, prev_a, *kept = join([out_sum, up_sum, down_sum], r4, r5, prev_a, *kept)
    n_a = send(prev_a, back, "fsdp")
    out_sum.swap()
    *kept, prev_b = attend_back(place, doc_row, lse, new, old, cots, half, half, kept)
    n_a, prev_b, *kept = join([out_sum, down_sum], n_a, prev_b, *kept)
    n_b = send(prev_b, back, "fsdp")
    grad_q, own_k, own_v = kept
    out_sum.split()
    down_sum.refine()
    (n_b,) = join([out_sum, down_sum], n_b)

    def piece(rows):
        arrived = jnp.concatenate([n_a[:, rows], n_b[:, rows]], axis=2)
        return jnp.stack([grad_q[rows], add(own_k[rows], arrived[0]), add(own_v[rows], arrived[1])])

    def first_back(grad):
        return jnp.einsum("ste,sde->td", grad, full_qkv, preferred_element_type=f32).astype(bf)

    last = slice(3 * QB, 4 * QB)
    q3 = piece(last)
    p3 = first_back(q3)
    t1 = send(p3, INWARD)
    q012 = after(piece(slice(0, 3 * QB)), p3)
    p012 = first_back(q012)
    out_sum.parts = [after(p, p012) for p in out_sum.parts]
    down_sum.parts = [after(p, p012) for p in down_sum.parts]
    out_sum.spread()
    down_sum.finish()
    qkv_sum = GradSum(attn_rows, [(q012, 3, k) for k in range(3)] + [(q3, 3, 0)], True)
    qkv_sum.product(p3)
    t1, p012, p3 = join([qkv_sum, out_sum, down_sum], t1, p012, p3)
    p0, p1, p2 = [p012[k * QB : (k + 1) * QB] for k in range(3)]
    t2, t3 = send(p2, INWARD), send(add(p2, t1), MIDDLE)
    qkv_sum.swap()
    qkv_sum.split()
    qkv_sum.spread()
    late = tie(p0, p1, p2, p3, qkv_sum.back)[:4]
    gain_one = functools.reduce(
        jnp.add,
        [jnp.sum(p.astype(f32) * r.astype(f32), axis=0) for p, r in zip(late, attn_rows)],
    )
    gains = jnp.stack([gain_one / norm_gains[0], gain_two[0]])
    if lax.axis_size("fsdp") == 8:
        gains = [gains] + [send(gains, flip(k), "fsdp") for k in range(1, 8)]
    else:
        gains = [lax.psum(gains, "fsdp")]
    down_own = down_sum.own(False)
    up_own = up_sum.own(True, qkv_sum.back)
    t2, t3, down_own, up_own, *gains = tie(t2, t3, down_own, up_own, *gains)
    t4, t5 = send(add(p3, t2), MIDDLE), send(add(p1, t3), PAIRS)
    gains = total_of(*gains)
    out_own = out_sum.own(False, t2)
    layer_output = (
        residual_mid + (d0.astype(f32) + r4.astype(f32) + after(r5, t2).astype(f32))
    ).astype(bf)
    t4, t5, gains, layer_output, out_own = tie(t4, t5, gains, layer_output, out_own)
    gains = total_of(gains, *[send(gains, flip(k, "tp"), "tp") for k in (1, 2, 3)])
    (input_grad,) = norm_back(
        norm_gains[0], [p0, t4, t5], layer_input, inverse_one, grad_mid, False
    )
    qkv_own = qkv_sum.own(True, t5)
    return (layer_output, input_grad, gains, qkv_own, out_own[0], up_own, down_own[0])


def solution(mesh):
    in_specs = (
        P(("fsdp", "tp"), None),
        P(),
        P(None, "fsdp", "tp"),
        P("tp", "fsdp"),
        P(None, "fsdp", "tp"),
        P("tp", "fsdp"),
        P("fsdp"),
        P(("fsdp", "tp"), None),
    )
    out_specs = (
        P(("fsdp", "tp"), None),
        P(("fsdp", "tp"), None),
        P(),
        P(None, "fsdp", "tp"),
        P("tp", "fsdp"),
        P(None, "fsdp", "tp"),
        P("tp", "fsdp"),
    )
    return jax.shard_map(
        per_device, mesh=mesh, in_specs=in_specs, out_specs=out_specs, check_vma=False
    )
```

```python
import functools
import math

import jax
import jax.numpy as jnp
from jax import lax
from jax.experimental import pallas as pl
from jax.experimental.pallas import tpu as pltpu
from jax.sharding import PartitionSpec as P

HEAD_DIM = 128
WINDOW = 1024
SEQ_LEN = 4096
QB = 256
SCALE = 1.0 / math.sqrt(HEAD_DIM)
LOG2E = 1.4426950408889634
EPS = 1e-06
MASKED = -1e30
VMEM_LIMIT = 36 << 20
ATTEND_LIMIT = 60 << 20
SMALL = pl.CostEstimate(flops=1 << 20, bytes_accessed=1 << 16, transcendentals=0)
NT = (((1,), (1,)), ((), ()))
TN = (((0,), (0,)), ((), ()))


def nt(a, b):
    return lax.dot_general(a, b, NT, preferred_element_type=jnp.float32)


def nn(a, b):
    return jnp.dot(a, b, preferred_element_type=jnp.float32)


def tn(a, b):
    return lax.dot_general(a, b, TN, preferred_element_type=jnp.float32)


def masked_scores(k_j, q, j, lo):
    s = nt(k_j, q)
    row = lax.broadcasted_iota(jnp.int32, s.shape, 0) + j * QB
    ok = row >= lo
    if (j + 1) * QB > WINDOW:
        hi = lax.broadcasted_iota(jnp.int32, (1, QB), 1) + WINDOW
        ok = ok & (row <= hi)
    return jnp.where(ok, s, MASKED)


def low_bound(doc_ref, b, off):
    q_row = lax.broadcasted_iota(jnp.int32, (1, QB), 1)
    doc = doc_ref[:, b * QB : (b + 1) * QB]
    return jnp.maximum(q_row + 1, doc - off + (WINDOW - b * QB))


def block_at(index):
    return pl.ds(pl.multiple_of(index * QB, QB), QB)


def attend_kernel(place_ref, doc_ref, *refs):
    new, old = refs[:4], refs[4:8]
    o_ref, lse_ref, q_s, k_s, vt_s = refs[8:]
    h = pl.program_id(0)
    off, me = place_ref[0], place_ref[1]
    blocks = len(new)
    for slot in range(blocks):
        at = me ^ slot
        q_s[block_at(at)] = new[slot][0]
        k_s[block_at(at)] = old[slot][0]
        k_s[block_at(at + blocks)] = new[slot][1]
        vt_s[:, block_at(at)] = old[slot][1].T
        vt_s[:, block_at(at + blocks)] = new[slot][2].T
    c = SCALE * LOG2E
    n = WINDOW // QB + 1
    for b in range(blocks):
        q = q_s[b * QB : (b + 1) * QB]
        lo = low_bound(doc_ref, b, off)
        ss = [
            masked_scores(k_s[(b + j) * QB : (b + j + 1) * QB], q, j, lo) for j in range(n)
        ]
        m = functools.reduce(jnp.maximum, [jnp.max(s, axis=0, keepdims=True) for s in ss])
        total = jnp.zeros((1, QB), jnp.float32)
        acc = jnp.zeros((HEAD_DIM, QB), jnp.float32)
        for j in range(n):
            p = jnp.exp2((ss[j] - m) * c)
            total = total + jnp.sum(p, axis=0, keepdims=True)
            acc = acc + nn(vt_s[:, (b + j) * QB : (b + j + 1) * QB], p.astype(jnp.bfloat16))
        o_ref[block_at(me ^ b)] = (acc / total).T.astype(o_ref.dtype)
        lse_ref[pl.ds(h, 1), b * QB : (b + 1) * QB] = m * c + jnp.log2(total)


def back_kernel(first, place_ref, doc_ref, lse_ref, *refs):
    new, old, cot = refs[:4], refs[4:8], refs[8:12]
    dq_ref, dk_ref, dv_ref, prev_ref, q_s, do_s, k_s, v_s, kt_s, dk_s, dv_s = refs[-11:]
    h = pl.program_id(0)
    off, me = place_ref[0], place_ref[1]
    blocks = len(new)
    for slot in range(blocks):
        at = me ^ slot
        q_s[block_at(at)] = new[slot][0]
        do_s[block_at(at)] = cot[slot][...]
        k_s[block_at(at)] = old[slot][0]
        k_s[block_at(at + blocks)] = new[slot][1]
        v_s[block_at(at)] = old[slot][1]
        v_s[block_at(at + blocks)] = new[slot][2]
        kt_s[:, block_at(at)] = old[slot][0].T
        kt_s[:, block_at(at + blocks)] = new[slot][1].T
    c = SCALE * LOG2E
    n = WINDOW // QB + 1
    seen = 0
    for b in range(blocks):
        q = q_s[b * QB : (b + 1) * QB]
        do = do_s[b * QB : (b + 1) * QB]
        lse = lse_ref[pl.ds(h + first, 1), b * QB : (b + 1) * QB]
        lo = low_bound(doc_ref, b, off)
        delta = jnp.zeros((1, QB), jnp.float32)
        ps, dps = [], []
        for j in range(n):
            rows = slice((b + j) * QB, (b + j + 1) * QB)
            p = jnp.exp2(masked_scores(k_s[rows], q, j, lo) * c - lse)
            dp = nt(v_s[rows], do)
            delta = delta + jnp.sum(p * dp, axis=0, keepdims=True)
            dv = nn(p.astype(jnp.bfloat16), do)
            if b + j >= seen:
                dv_s[rows] = dv
            else:
                dv_s[rows] += dv
            ps.append(p)
            dps.append(dp)
        dqt = jnp.zeros((HEAD_DIM, QB), jnp.float32)
        for j in range(n):
            rows = slice((b + j) * QB, (b + j + 1) * QB)
            ds = (ps[j] * (dps[j] - delta)).astype(jnp.bfloat16)
            dk = nn(ds, q)
            if b + j >= seen:
                dk_s[rows] = dk
            else:
                dk_s[rows] += dk
            dqt = dqt + nn(kt_s[:, rows], ds)
        seen = b + n
        dq_ref[block_at(me ^ b)] = (dqt * SCALE).T.astype(dq_ref.dtype)
    for slot in range(blocks):
        at = me ^ slot
        rows = slice(slot * QB, (slot + 1) * QB)
        prev_ref[0, rows] = (dk_s[block_at(at)] * SCALE).astype(prev_ref.dtype)
        prev_ref[1, rows] = dv_s[block_at(at)].astype(prev_ref.dtype)
        dk_ref[rows] = dk_s[block_at(at + blocks)] * SCALE
        dv_ref[rows] = dv_s[block_at(at + blocks)]


def spec2(rows, first=0):
    return pl.BlockSpec((rows, HEAD_DIM), lambda h: (0, h + first))


def spec3(count, rows, first=0):
    return pl.BlockSpec((count, rows, HEAD_DIM), lambda h: (0, 0, h + first))


def constant(shape):
    return pl.BlockSpec(shape, lambda h: (0, 0))


def attend(place, doc, new, old):
    blocks = len(new)
    span, width = blocks * QB, new[0].shape[-1]
    heads = width // HEAD_DIM
    bf = jnp.bfloat16
    return pl.pallas_call(
        attend_kernel,
        grid=(heads,),
        in_specs=[pl.BlockSpec(memory_space=pltpu.SMEM), constant((1, span))]
        + [spec3(3, QB)] * blocks
        + [spec3(2, QB)] * blocks,
        out_specs=[spec2(span), constant((heads, span))],
        out_shape=[
            jax.ShapeDtypeStruct((span, width), bf),
            jax.ShapeDtypeStruct((heads, span), jnp.float32),
        ],
        scratch_shapes=[
            pltpu.VMEM((span, HEAD_DIM), bf),
            pltpu.VMEM((WINDOW + span, HEAD_DIM), bf),
            pltpu.VMEM((HEAD_DIM, WINDOW + span), bf),
        ],
        compiler_params=pltpu.CompilerParams(vmem_limit_bytes=ATTEND_LIMIT),
        cost_estimate=SMALL,
    )(place, doc, *new, *old)


def attend_back(place, doc, lse, new, old, cot, first, heads, kept=()):
    blocks = len(new)
    span, width = blocks * QB, new[0].shape[-1]
    bf, f32 = jnp.bfloat16, jnp.float32
    fixed = 3 + 3 * blocks
    return pl.pallas_call(
        functools.partial(back_kernel, first),
        grid=(heads,),
        in_specs=[
            pl.BlockSpec(memory_space=pltpu.SMEM),
            constant((1, span)),
            constant(lse.shape),
        ]
        + [spec3(3, QB, first)] * blocks
        + [spec3(2, QB, first)] * blocks
        + [spec2(QB, first)] * blocks
        + [pl.BlockSpec(memory_space=pl.ANY)] * len(kept),
        out_specs=[spec2(span, first)] * 3 + [spec3(2, WINDOW)],
        out_shape=[
            jax.ShapeDtypeStruct((span, width), bf),
            jax.ShapeDtypeStruct((span, width), f32),
            jax.ShapeDtypeStruct((span, width), f32),
            jax.ShapeDtypeStruct((2, WINDOW, heads * HEAD_DIM), bf),
        ],
        input_output_aliases={fixed + i: i for i in range(len(kept))},
        scratch_shapes=[pltpu.VMEM((span, HEAD_DIM), bf)] * 2
        + [pltpu.VMEM((WINDOW + span, HEAD_DIM), bf)] * 2
        + [pltpu.VMEM((HEAD_DIM, WINDOW + span), bf)]
        + [pltpu.VMEM((WINDOW + span, HEAD_DIM), f32)] * 2,
        compiler_params=pltpu.CompilerParams(vmem_limit_bytes=ATTEND_LIMIT),
        cost_estimate=SMALL,
    )(place, doc, lse, *new, *old, *cot, *kept)


PAIRS = [(0, 1), (1, 0), (2, 3), (3, 2)]
MIDDLE = [(1, 2), (2, 1)]
OUTWARD = [(1, 0), (2, 3)]
INWARD = [(0, 1), (3, 2)]


def send(block, route, axis="tp"):
    return lax.ppermute(block, axis, route)


def tie(*values):
    return lax.optimization_barrier(values)


def after(value, *others):
    return lax.optimization_barrier((value,) + others)[0]


def flip(bit, axis="fsdp"):
    return [(i, i ^ bit) for i in range(lax.axis_size(axis))]


def neighbour_route(distance, per_seq):
    size = lax.axis_size("fsdp")
    pairs = [(i - 1, i) for i in range(1, size) if i % per_seq]
    return pairs if distance > 0 else [(b, a) for a, b in pairs]


def pick(array, index, axis):
    return lax.dynamic_index_in_dim(array, index, axis, keepdims=False)


NORM_ROWS = 64


def row_mean(values):
    return jnp.mean(values, axis=-1, keepdims=True)


def total_of(first, *more):
    total = first.astype(jnp.float32)
    for array in more:
        total = total + array.astype(jnp.float32)
    return total


def norm_kernel(parts, gain_ref, *refs):
    total = total_of(*[ref[...] for ref in refs[:parts]])
    inverse = lax.rsqrt(row_mean(total * total) + EPS)
    refs[parts][...] = (total * inverse * gain_ref[...]).astype(jnp.bfloat16)
    refs[parts + 1][...] = jnp.broadcast_to(inverse, refs[parts + 1].shape)
    if len(refs) > parts + 2:
        refs[parts + 2][...] = total


def row_call(kernel, gain, arrays, outs, sums=0):
    rows, width = arrays[0].shape
    block = lambda w: pl.BlockSpec((NORM_ROWS, w), lambda r: (r, 0))
    one = pl.BlockSpec((1, width), lambda r: (0, 0))
    return pl.pallas_call(
        kernel,
        grid=(rows // NORM_ROWS,),
        in_specs=[one] + [block(a.shape[1]) for a in arrays],
        out_specs=[block(w) for w, _ in outs] + [one] * sums,
        out_shape=[jax.ShapeDtypeStruct((rows, w), t) for w, t in outs]
        + [jax.ShapeDtypeStruct((1, width), jnp.float32)] * sums,
        compiler_params=pltpu.CompilerParams(vmem_limit_bytes=VMEM_LIMIT),
        cost_estimate=SMALL,
    )(gain[None], *arrays)


def norm(gain, parts, keep):
    width = parts[0].shape[1]
    outs = [(width, jnp.bfloat16), (128, jnp.float32)] + [(width, jnp.float32)] * keep
    return row_call(functools.partial(norm_kernel, len(parts)), gain, parts, outs)


def norm_back_kernel(parts, gain_ref, *refs):
    grad = total_of(*[ref[...] for ref in refs[:parts]])
    value_ref, inverse_ref, more_ref = refs[parts : parts + 3]
    outs = refs[parts + 3 :]
    inverse = inverse_ref[:, :1]
    unit = value_ref[...].astype(jnp.float32) * inverse
    scaled = grad * gain_ref[...]
    result = more_ref[...].astype(jnp.float32) + inverse * (
        scaled - unit * row_mean(scaled * unit)
    )
    outs[0][...] = result.astype(jnp.bfloat16)
    if len(outs) == 3:
        outs[1][...] = result

        @pl.when(pl.program_id(0) == 0)
        def _():
            outs[2][...] = jnp.zeros_like(outs[2])

        outs[2][...] += jnp.sum(grad * unit, axis=0, keepdims=True)


def norm_back(gain, parts, value, inverse, more, keep):
    width = value.shape[1]
    outs = [(width, jnp.bfloat16)] + [(width, jnp.float32)] * keep
    return row_call(
        functools.partial(norm_back_kernel, len(parts)),
        gain,
        [*parts, value, inverse, more],
        outs,
        sums=int(keep),
    )


def add(a, b):
    return (a.astype(jnp.float32) + b.astype(jnp.float32)).astype(jnp.bfloat16)


def grad_kernel(blocks, which_ref, *refs):
    lhs, rhs = refs[:blocks], refs[blocks : 2 * blocks]
    away_ref, kept_ref, lhs_s, rhs_s = refs[2 * blocks :]
    count, e = away_ref.shape[1:3]
    group, groups = pl.program_id(0), pl.num_programs(0) // 2

    @pl.when(group == 0)
    def _():
        for k in range(blocks):
            for s in range(count):
                rhs_s[s * e : (s + 1) * e, k * QB : (k + 1) * QB] = rhs[k][s].T

    for k in range(blocks):
        lhs_s[k * QB : (k + 1) * QB] = lhs[k][...]

    def product(out_ref):
        for s in range(count):
            out_ref[0, s] = nn(rhs_s[s * e : (s + 1) * e], lhs_s[...]).astype(out_ref.dtype)

    pl.when(group < groups)(lambda: product(away_ref))
    pl.when(group >= groups)(lambda: product(kept_ref))


def grad_product(own, lhs, rhs):
    blocks = len(lhs)
    e = rhs[0][0].shape[-1]
    count = rhs[0][1]
    groups = lhs[0].shape[1] // (2 * QB)

    def lhs_at(j, own):
        parity = jnp.where(j < groups, 1 - own[0], own[0])
        return (0, 2 * lax.rem(j, groups) + parity)

    def rhs_at(array, k):
        at = (0, k, 0) if array.shape[0] == count else (k, 0, 0)
        return pl.BlockSpec((count, QB, e), lambda j, own: at)

    out = jax.ShapeDtypeStruct((groups, count, e, QB), jnp.bfloat16)
    return pl.pallas_call(
        functools.partial(grad_kernel, blocks),
        grid_spec=pltpu.PrefetchScalarGridSpec(
            num_scalar_prefetch=1,
            grid=(2 * groups,),
            in_specs=[pl.BlockSpec((QB, QB), lhs_at)] * blocks
            + [rhs_at(array, k) for array, _, k in rhs],
            out_specs=[
                pl.BlockSpec(
                    (1, count, e, QB), lambda j, own: (jnp.minimum(j, groups - 1), 0, 0, 0)
                ),
                pl.BlockSpec((1, count, e, QB), lambda j, own: (jnp.maximum(j - groups, 0), 0, 0, 0)),
            ],
            scratch_shapes=[
                pltpu.VMEM((blocks * QB, QB), jnp.bfloat16),
                pltpu.VMEM((count * e, blocks * QB), jnp.bfloat16),
            ],
        ),
        out_shape=[out, out],
        compiler_params=pltpu.CompilerParams(vmem_limit_bytes=ATTEND_LIMIT if count == 2 else VMEM_LIMIT),
        cost_estimate=SMALL,
    )(own.reshape(1).astype(jnp.int32), *lhs, *[r[0] for r in rhs])


def turn_kernel(group_ref, kept_ref, back_ref, *refs):
    total = kept_ref[0, 0].astype(jnp.float32) + back_ref[0, 0].astype(jnp.float32)
    for ref in refs[:-1]:
        total = total + ref[0].astype(jnp.float32)
    refs[-1][0] = total.T


def turn(group, kept, back, parts):
    groups, count, e, width = kept.shape
    mine = pl.BlockSpec((1, 1, e, width), lambda s, group: (group[0], s, 0, 0))
    return pl.pallas_call(
        turn_kernel,
        grid_spec=pltpu.PrefetchScalarGridSpec(
            num_scalar_prefetch=1,
            grid=(count,),
            in_specs=[mine, mine]
            + [pl.BlockSpec((1, e, width), lambda s, group: (s, 0, 0))] * len(parts),
            out_specs=pl.BlockSpec((1, width, e), lambda s, group: (s, 0, 0)),
        ),
        out_shape=jax.ShapeDtypeStruct((count, width, e), jnp.float32),
        compiler_params=pltpu.CompilerParams(vmem_limit_bytes=VMEM_LIMIT),
        cost_estimate=SMALL,
    )(group.reshape(1).astype(jnp.int32), kept, back, *parts)


def rows_kernel(blocks, *refs):
    w_ref, out_ref = refs[blocks], refs[blocks + 1]
    for k in range(blocks):
        out_ref[k * QB : (k + 1) * QB] = nn(refs[k][...], w_ref[...]).astype(out_ref.dtype)


def rows_product(lhs, w):
    blocks, inner, cols = len(lhs), w.shape[0], w.shape[1]
    wide = 512
    return pl.pallas_call(
        functools.partial(rows_kernel, blocks),
        grid=(cols // wide,),
        in_specs=[pl.BlockSpec((QB, inner), lambda n: (0, 0))] * blocks
        + [pl.BlockSpec((inner, wide), lambda n: (0, n))],
        out_specs=pl.BlockSpec((blocks * QB, wide), lambda n: (0, n)),
        out_shape=jax.ShapeDtypeStruct((blocks * QB, cols), jnp.bfloat16),
        compiler_params=pltpu.CompilerParams(vmem_limit_bytes=VMEM_LIMIT),
        cost_estimate=SMALL,
    )(*lhs, w)


class GradSum:
    def __init__(self, lhs, rhs, direct):
        me = lax.axis_index("fsdp")
        self.low, self.one, self.two = me % 2, (me // 2) % 2, me // 4
        self.group = me // 2
        self.lhs, self.rhs, self.direct = lhs, rhs, direct
        self.staged = lax.axis_size("fsdp") == 8
        self.back, self.parts = jnp.zeros((), jnp.bfloat16), []

    def product(self, *others):
        own = self.low if self.staged else jnp.int32(1)
        self.away, self.kept = grad_product(after(own, *others), self.lhs, self.rhs)

    def swap(self):
        if self.staged:
            self.back = send(self.away, flip(1), "fsdp")

    def half(self, index, axis, top, *more):
        groups, s, e, width = self.kept.shape
        start, size = [0] * 5, [2, 2, s, e // 2, width]
        start[axis], size[axis] = index, 1
        start[3] = 0 if top else e // 2
        cuts = [
            jnp.squeeze(lax.dynamic_slice(a.reshape(2, 2, s, e, width), start, size), axis)
            for a in (self.kept, self.back)
        ]
        return total_of(*cuts, *more).astype(jnp.bfloat16)

    def split(self):
        if self.staged and self.direct:
            self.parts = [
                total_of(pick(self.kept, self.group ^ k, 0), pick(self.back, self.group ^ k, 0))
                for k in (1, 2, 3)
            ]
            self.parts = [part.astype(jnp.bfloat16) for part in self.parts]
        elif self.staged:
            self.parts = [self.half(1 - self.one, 1, True), self.half(1 - self.two, 0, False)]

    def spread(self):
        routes = (2, 4, 6) if self.direct else (2, 4)
        self.parts = [send(p, flip(r), "fsdp") for p, r in zip(self.parts, routes)]

    def refine(self):
        if self.staged:
            self.a = self.half(self.one, 1, True, self.parts[0])
            self.b = self.half(self.two, 0, False, self.parts[1])
            self.parts = [pick(self.a, 1 - self.two, 0), pick(self.b, 1 - self.one, 0)]

    def finish(self):
        self.parts = [send(p, flip(r), "fsdp") for p, r in zip(self.parts, (4, 2))]

    def own(self, turned, *others):
        if not self.staged:
            both = jnp.stack([self.away, self.kept], axis=1)
            groups, _, s, e, width = both.shape
            both = both.transpose(2, 3, 0, 1, 4).reshape(s, e, 2 * groups * width)
            own = lax.psum_scatter(both, "fsdp", scatter_dimension=2, tiled=True)
            own = own.astype(jnp.float32)
            return own.transpose(0, 2, 1) if turned else own
        parts = tie(*self.parts, *others)[: len(self.parts)]
        if not self.direct:
            top = total_of(pick(self.a, self.two, 0), parts[0])
            bottom = total_of(pick(self.b, self.one, 0), parts[1])
            own = jnp.concatenate([top, bottom], axis=1)
            return own.transpose(0, 2, 1) if turned else own
        if turned:
            return turn(self.group, self.kept, self.back, parts)
        return total_of(pick(self.kept, self.group, 0), pick(self.back, self.group, 0), *parts)


def join(sums, *values):
    held = [[s.away, s.kept, s.back, *s.parts] for s in sums]
    tied = list(tie(*values, *[h for hs in held for h in hs]))
    out, tied = tied[: len(values)], tied[len(values) :]
    for s, hs in zip(sums, held):
        s.away, s.kept, s.back, *s.parts = tied[: len(hs)]
        tied = tied[len(hs) :]
    return out


def per_device(layer_input, norm_gains, w_qkv, w_out, w_gate_up, w_down, doc_start, out_cotangent):
    bf, f32 = jnp.bfloat16, jnp.float32
    span_len = doc_start.shape[0]
    me = lax.axis_index("tp")
    mid = (me == 1) | (me == 2)
    per_seq = SEQ_LEN // span_len
    place = jnp.stack([lax.axis_index("fsdp") * span_len, me]).astype(jnp.int32)
    doc_row = doc_start.reshape(1, span_len)
    full_qkv = lax.all_gather(w_qkv, "fsdp", axis=1, tiled=True)
    full_out = lax.all_gather(w_out, "fsdp", axis=1, tiled=True)
    forth, back = neighbour_route(1, per_seq), neighbour_route(-1, per_seq)

    normed_one, inverse_one = norm(norm_gains[0], [layer_input], False)
    xm, x1 = send(normed_one, MIDDLE), send(normed_one, PAIRS)
    xo, xf = send(xm, OUTWARD), send(x1, MIDDLE)
    full_qkv = after(full_qkv, x1)

    def project(block):
        return jnp.einsum("td,sde->ste", block, full_qkv, preferred_element_type=f32).astype(bf)

    first = project(normed_one)
    xf, xo, first = tie(xf, xo, first)
    x2 = jnp.where(mid, xf, xo)
    x3 = send(xf, OUTWARD)
    attn_rows = [normed_one, x1, x2]
    new = [first, project(x1), project(x2)]
    old = [send(n[1:], forth, "fsdp") for n in new]
    x3, *old = tie(x3, *old)
    attn_rows.append(jnp.where(mid, xm, x3))
    new.append(project(attn_rows[3]))
    old.append(send(new[3][1:], forth, "fsdp"))
    old[3], w_gate_up, w_down = tie(old[3], w_gate_up, w_down)
    full_gate_up = lax.all_gather(w_gate_up, "fsdp", axis=1, tiled=True)
    full_down = lax.all_gather(w_down, "fsdp", axis=1, tiled=True)
    late_cot = after(out_cotangent, new[3])
    c1, cm = send(late_cot, PAIRS), send(late_cot, MIDDLE)
    heads_out, lse = attend(place, doc_row, new, old)

    def out_part(k):
        return nn(heads_out[k * QB : (k + 1) * QB], full_out).astype(bf)

    def cross(middle, end):
        return send(jnp.where(mid, middle, end), PAIRS)

    a3 = out_part(3)
    y1 = cross(after(cm, a3), a3)
    c1 = after(c1, a3)
    cf = send(c1, MIDDLE)
    a2, a1, a0 = out_part(2), out_part(1), out_part(0)
    y1, cf, a2, a1, a0 = tie(y1, cf, a2, a1, a0)
    y2, t3 = cross(cf, a2), send(add(a2, y1), MIDDLE)
    y2, t3 = tie(y2, t3)
    t4, t5 = send(add(a3, y2), MIDDLE), send(add(a1, t3), PAIRS)
    cot = [out_cotangent, c1, jnp.where(mid, cf, y1), jnp.where(mid, cm, y2)]
    t4, t5 = tie(t4, t5)
    normed_two, inverse_two, residual_mid = norm(norm_gains[1], [layer_input, a0, t4, t5], True)

    def up(rows):
        return jnp.einsum("td,sdf->stf", rows, full_gate_up, preferred_element_type=f32)

    def down(gate_up, cot_rows):
        gate_pre, up_pre = gate_up[0], gate_up[1]
        sig = jax.nn.sigmoid(gate_pre)
        act = (gate_pre * sig * up_pre).astype(bf)
        grad_act = nt(cot_rows, full_down)
        grad_up = grad_act * gate_pre * sig
        grad_gate = grad_act * up_pre * sig * (1.0 + gate_pre * (1.0 - sig))
        return act, jnp.stack([grad_gate, grad_up]).astype(bf)

    def second_back(grads):
        return jnp.einsum("stf,sdf->td", grads, full_gate_up, preferred_element_type=f32).astype(bf)

    m1, mm = send(normed_two, PAIRS), send(normed_two, MIDDLE)
    u0 = up(normed_two)
    m1, mm, u0 = tie(m1, mm, u0)
    mo, mf = send(mm, OUTWARD), send(m1, MIDDLE)
    u1 = up(m1)
    f0 = down(after(u0, u1), cot[0])
    mf, mo, u1, f0 = tie(mf, mo, u1, f0)
    m2 = jnp.where(mid, mf, mo)
    m3 = send(mf, OUTWARD)
    f1 = down(u1, cot[1])
    f2 = down(up(m2), cot[2])
    g0, g1, g2 = second_back(f0[1]), second_back(f1[1]), second_back(f2[1])
    m3, f1, f2, g0, g1, g2 = tie(m3, f1, f2, g0, g1, g2)
    m3 = jnp.where(mid, mm, m3)
    f3 = down(up(m3), cot[3])
    g3 = second_back(f3[1])

    feed = (f0, f1, f2, f3)
    t1 = send(g3, INWARD)
    up_sum = GradSum([normed_two, m1, m2, m3], [(f[1], 2, 0) for f in feed], False)
    up_sum.product(g3)
    (t1,) = join([up_sum], t1)
    t2, t3 = send(after(g2, t1), INWARD), send(add(g2, t1), MIDDLE)
    up_sum.swap()
    down_sum = GradSum(cot, [(f[0][None], 1, 0) for f in feed], False)
    down_sum.product(t1)
    t2, t3 = join([up_sum, down_sum], t2, t3)
    t4, t5 = send(add(g3, t2), MIDDLE), send(add(g1, t3), PAIRS)
    down_sum.swap()
    up_sum.split()
    down_part = rows_product([f[0] for f in feed[:3]] + [after(f3[0], t2)], full_down)
    t4, t5, down_part = join([up_sum, down_sum], t4, t5, down_part)
    grad_branch, grad_mid, gain_two = norm_back(
        norm_gains[1], [g0, t4, t5], residual_mid, inverse_two, out_cotangent, True
    )

    def heads_back(block):
        return nt(block, full_out).astype(bf)

    d3, d2, d1, d0 = [down_part[k * QB : (k + 1) * QB] for k in (3, 2, 1, 0)]
    b1, bm = send(grad_branch, PAIRS), send(grad_branch, MIDDLE)
    up_sum.spread()
    down_sum.kept = after(down_sum.kept, grad_branch)
    down_sum.split()
    h0 = heads_back(grad_branch)
    b1, bm, h0 = join([down_sum], b1, bm, h0)
    y1, bfar = cross(bm, d3), send(b1, MIDDLE)
    down_sum.spread()
    h1 = heads_back(b1)
    y1, bfar, h1 = join([up_sum], y1, bfar, h1)
    b2 = jnp.where(mid, bfar, y1)
    y2, r3 = cross(bfar, d2), send(add(d2, y1), MIDDLE)
    up_sum.refine()
    h2 = heads_back(b2)
    y2, r3, h2 = join([up_sum, down_sum], y2, r3, h2)
    b3 = jnp.where(mid, bm, y2)
    h3 = heads_back(b3)
    r4, r5 = send(add(d3, y2), MIDDLE), send(add(d1, r3), PAIRS)
    up_sum.finish()
    cots = [h0, h1, h2, h3]
    half = heads_out.shape[1] // HEAD_DIM // 2
    *kept, prev_a = attend_back(place, doc_row, lse, new, old, cots, 0, half)
    head_blocks = heads_out.reshape(4, QB, -1)
    gb_blocks = [grad_branch, b1, b2, b3]
    out_sum = GradSum(gb_blocks, [(head_blocks, 1, k) for k in range(4)], True)
    out_sum.product(h3)
    r4, r5, prev_a, *kept = join([out_sum, up_sum, down_sum], r4, r5, prev_a, *kept)
    n_a = send(prev_a, back, "fsdp")
    out_sum.swap()
    *kept, prev_b = attend_back(place, doc_row, lse, new, old, cots, half, half, kept)
    n_a, prev_b, *kept = join([out_sum, down_sum], n_a, prev_b, *kept)
    n_b = send(prev_b, back, "fsdp")
    grad_q, own_k, own_v = kept
    out_sum.split()
    down_sum.refine()
    (n_b,) = join([out_sum, down_sum], n_b)

    def piece(rows):
        arrived = jnp.concatenate([n_a[:, rows], n_b[:, rows]], axis=2)
        return jnp.stack([grad_q[rows], add(own_k[rows], arrived[0]), add(own_v[rows], arrived[1])])

    def first_back(grad):
        return jnp.einsum("ste,sde->td", grad, full_qkv, preferred_element_type=f32).astype(bf)

    last = slice(3 * QB, 4 * QB)
    q3 = piece(last)
    p3 = first_back(q3)
    t1 = send(p3, INWARD)
    out_sum.parts = [after(p, p3) for p in out_sum.parts]
    down_sum.parts = [after(p, p3) for p in down_sum.parts]
    out_sum.spread()
    down_sum.finish()
    q012 = after(piece(slice(0, 3 * QB)), p3)
    p012 = first_back(q012)
    qkv_sum = GradSum(attn_rows, [(q012, 3, k) for k in range(3)] + [(q3, 3, 0)], True)
    qkv_sum.product(p3)
    t1, p012, p3 = join([qkv_sum, out_sum, down_sum], t1, p012, p3)
    p0, p1, p2 = [p012[k * QB : (k + 1) * QB] for k in range(3)]
    t2, t3 = send(p2, INWARD), send(add(p2, t1), MIDDLE)
    qkv_sum.swap()
    qkv_sum.split()
    qkv_sum.spread()
    late = tie(p0, p1, p2, p3, qkv_sum.back)[:4]
    gain_one = functools.reduce(
        jnp.add,
        [jnp.sum(p.astype(f32) * r.astype(f32), axis=0) for p, r in zip(late, attn_rows)],
    )
    gains = jnp.stack([gain_one / norm_gains[0], gain_two[0]])
    if lax.axis_size("fsdp") == 8:
        gains = [gains] + [send(gains, flip(k), "fsdp") for k in range(1, 8)]
    else:
        gains = [lax.psum(gains, "fsdp")]
    down_own = down_sum.own(False)
    up_own = up_sum.own(True, qkv_sum.back)
    t2, t3, down_own, up_own, *gains = tie(t2, t3, down_own, up_own, *gains)
    t4, t5 = send(add(p3, t2), MIDDLE), send(add(p1, t3), PAIRS)
    gains = total_of(*gains)
    out_own = out_sum.own(False, t2)
    layer_output = (
        residual_mid + (d0.astype(f32) + r4.astype(f32) + after(r5, t2).astype(f32))
    ).astype(bf)
    t4, t5, gains, layer_output, out_own = tie(t4, t5, gains, layer_output, out_own)
    gains = total_of(gains, *[send(gains, flip(k, "tp"), "tp") for k in (1, 2, 3)])
    (input_grad,) = norm_back(
        norm_gains[0], [p0, t4, t5], layer_input, inverse_one, grad_mid, False
    )
    qkv_own = qkv_sum.own(True, t5)
    return (layer_output, input_grad, gains, qkv_own, out_own[0], up_own, down_own[0])


def solution(mesh):
    in_specs = (
        P(("fsdp", "tp"), None),
        P(),
        P(None, "fsdp", "tp"),
        P("tp", "fsdp"),
        P(None, "fsdp", "tp"),
        P("tp", "fsdp"),
        P("fsdp"),
        P(("fsdp", "tp"), None),
    )
    out_specs = (
        P(("fsdp", "tp"), None),
        P(("fsdp", "tp"), None),
        P(),
        P(None, "fsdp", "tp"),
        P("tp", "fsdp"),
        P(None, "fsdp", "tp"),
        P("tp", "fsdp"),
    )
    return jax.shard_map(
        per_device, mesh=mesh, in_specs=in_specs, out_specs=out_specs, check_vma=False
    )
```
